256 devices in a mesh: band: 32 (over z, x), plane: 8 (over y, core).
Axes of the slice: x: 4, y: 4, z: 8, core: 2. Of those that a mesh axis runs over, the one named last changes fastest.
Arguments:
- stick_coef: float32 [480, 61440], P('plane', 'band'), may hold values from -6 to 6
- stick_list: int32 [480], P('plane'), may hold values from -1 to 239, as said below
Outputs:
- exch_field: float32 [256, 240, 240], P(('band', 'plane'))
The draws below stay inside these ranges and needn't reach their ends.
Inputs may be any that keep to these rules, and one draw needn't show every extreme that they name: `stick_list`: every stick 0 to 239 appears exactly once in the whole list. Each index of plane holds 60 consecutive entries, its live sticks first and -1 after them; one index holds exactly 60 live sticks and the others share the rest about evenly.
All inputs are finite; a program needn't handle non-finite values.
Results may differ from the reference program's by a relative error of at most 0.0003.
Values sent between devices are 32-bit elements; how exact they have to be, the bound alone decides.
A program may use at most 64 MiB of HBM per device.

```python
import math
import jax
import jax.numpy as jnp
from jax import lax

NX = 240
NY = 240
BLK = 8
ITERS = 4
NB = 256
SMAX = 60
SLOTS = 480
N_BAND = 32
N_PLANE = 8


def draw_stick_list(key, part):
    key = jax.random.fold_in(key, 11)
    first_key, second_key = jax.random.split(key)
    ordering = jax.random.permutation(first_key, NY).astype(jnp.int32)
    busiest = jax.random.randint(second_key, (), 0, N_PLANE).astype(jnp.int32)
    remaining = NY - SMAX
    others = N_PLANE - 1
    ranking = (jnp.arange(N_PLANE, dtype=jnp.int32) - busiest - 1) % N_PLANE
    spread = remaining * (ranking + 1) // others - remaining * ranking // others
    counts = jnp.where(ranking == others, SMAX, spread).astype(jnp.int32)
    starts = jnp.cumsum(counts) - counts
    slot_ids = jnp.arange(SMAX, dtype=jnp.int32)
    positions = jnp.clip(starts[:, None] + slot_ids[None, :], 0, NY - 1)
    live = slot_ids[None, :] < counts[:, None]
    values = jnp.where(live, ordering[positions], -1)
    return values.reshape(-1).astype(jnp.int32)


def level_of(stream_key, dims, cuts, least, high):
    level = 1.0
    for position, shards_of in cuts:
        steps = jax.random.uniform(jax.random.fold_in(jax.random.fold_in(stream_key, 6), position), (shards_of,), jnp.float32, least / len(cuts), high / len(cuts))
        level = level * jnp.repeat(jnp.exp(steps), dims[position] // shards_of).reshape((-1,) + (1,) * (len(dims) - 1 - position))
    return level


def scatter_about(stream_key, shape, scale, bound, cuts=(), held_as=jnp.bfloat16):
    level = level_of(stream_key, shape, cuts, -0.22, 0.18) if cuts else 1.0
    drawn = jax.random.normal(stream_key, shape, jnp.float32) * scale * level
    return jnp.minimum(jnp.maximum(drawn, -bound), bound).astype(held_as)


def setup_inputs(seed: int = 0) -> dict:
    streams_of = jax.random.split(jax.random.key(seed), 3)
    stick_coef = scatter_about(streams_of[0], (SLOTS, NB * NX), 1.0, 6.0, ((0, 8), (1, 32)), jnp.float32)
    stick_list = draw_stick_list(jax.random.fold_in(streams_of[2], 71), 0)
    return dict(stick_coef=stick_coef, stick_list=stick_list)


def hartley_axis(values, axis_number, extent):
    spectrum = jnp.fft.fft(values, axis=axis_number)
    return (spectrum.real - spectrum.imag) / math.sqrt(extent)

def coulomb_half():
    rows_freq = jnp.arange(NX, dtype=jnp.int32)
    rows_freq = jnp.minimum(rows_freq, NX - rows_freq).astype(jnp.float32)
    cols_freq = jnp.arange(NY // 2 + 1, dtype=jnp.int32).astype(jnp.float32)
    squared = rows_freq[:, None] * rows_freq[:, None] + cols_freq[None, :] * cols_freq[None, :]
    return jnp.where(squared > 0, 0.25 * NX / jnp.maximum(squared, 1.0), 0.0)

def reference(stick_coef, stick_list):
    targets = jnp.arange(NY, dtype=jnp.int32)
    selector = (stick_list[:, None] == targets[None, :]).astype(jnp.float32)
    shaped = stick_coef.astype(jnp.float32).reshape(SLOTS, NB, NX)
    spectra = jnp.einsum('sbk,sy->bky', shaped, selector, precision=lax.Precision.HIGHEST)
    orbitals = hartley_axis(hartley_axis(spectra, 1, NX), 2, NY)
    kernel = coulomb_half()

    def block_field(block_index):
        own_bands = lax.dynamic_slice_in_dim(orbitals, (block_index * BLK).astype(jnp.int32), BLK, 0)
        accumulated = jnp.zeros((BLK, NX, NY), orbitals.dtype)
        for loop_step in range(ITERS):
            source = ((block_index - loop_step) % N_BAND * BLK).astype(jnp.int32)
            partner = lax.dynamic_slice_in_dim(orbitals, source, BLK, 0)
            density = own_bands[:, None] * partner[None]
            potential = jnp.fft.irfft2(jnp.fft.rfft2(density) * kernel, s=(NX, NY))
            accumulated = accumulated + lax.optimization_barrier(jnp.sum(potential * partner[None], axis=1))
        return accumulated
    fields = lax.map(block_field, jnp.arange(N_BAND, dtype=jnp.int32))
    return fields.reshape(NB, NX, NY)
```

```python
import functools
import math

import jax
import jax.numpy as jnp
import ml_dtypes
import numpy as np
from jax import lax
from jax.experimental import pallas as pl
from jax.experimental.pallas import tpu as pltpu
from jax.sharding import PartitionSpec as P

N = 240
HALF = 128
FULL = 256
ROWS = 248
SLOTS = 60
CHUNK = 64
BANDS = 8
MESH = pl.DeviceIdType.MESH
F32 = jnp.float32
BF16 = jnp.bfloat16


def split_np(values):
    high = values.astype(np.float32).astype(ml_dtypes.bfloat16)
    low = (values - high.astype(np.float64)).astype(np.float32).astype(ml_dtypes.bfloat16)
    return high, low


def make_tables():
    spot = -np.ones(FULL, np.int64)
    spot[:121] = np.arange(121)
    spot[HALF + 1 : HALF + 120] = N - np.arange(1, 120)
    index = np.arange(N)
    phase = (index[:, None] * index[None, :] % N) * (2.0 * np.pi / N)
    hart = (np.cos(phase) + np.sin(phase)) / math.sqrt(N)
    folded = np.zeros((FULL, FULL))
    folded[spot >= 0, :N] = hart[spot[spot >= 0]]
    f_hi, f_lo = split_np(folded)
    hart_x = np.concatenate([f_hi, f_lo], 0)
    hart_y = np.concatenate([f_hi.T, f_lo.T], 1)
    cosine = np.zeros((HALF, HALF))
    cosine[:121, :121] = np.cos(phase[:121, :121]) / math.sqrt(N)
    sine = np.zeros((HALF, HALF))
    sine[1:120, 1:120] = np.sin(phase[1:120, 1:120]) / math.sqrt(N)
    right, left = [], []
    for table in (cosine, sine):
        hi, lo = split_np(table)
        right.append(np.block([[hi, lo], [hi, lo]]))
        left.append(np.block([[hi, hi], [lo, lo]]))
    freq = np.arange(HALF).astype(np.float64)
    weight = np.where((freq == 0) | (freq == 120), 1.0, 2.0)
    squared = freq[:, None] ** 2 + freq[None, :] ** 2
    coulomb = np.where(squared > 0, 0.25 * N / np.maximum(squared, 1.0), 0.0)
    coulomb = coulomb * weight[:, None] * weight[None, :]
    even = (freq <= 120).astype(np.float64)
    odd = ((freq >= 1) & (freq <= 119)).astype(np.float64)
    live = np.concatenate([even, odd])
    coulomb = (np.tile(coulomb, (2, 2)) * live[:, None] * live[None, :]).astype(np.float32)
    place = np.zeros((FULL, FULL), np.float32)
    for p in range(FULL):
        if spot[p] >= 0:
            place[p, spot[p]] = 1.0
    place_y = place.astype(ml_dtypes.bfloat16)
    place_x = place.T[:N].astype(ml_dtypes.bfloat16)
    return hart_x, hart_y, np.stack(right), np.stack(left), coulomb, place_x, place_y


def split(values):
    high = values.astype(BF16)
    low = (values - high.astype(F32)).astype(BF16)
    return high, low


def mm(lhs, rhs):
    return lax.dot_general(lhs, rhs, (((1,), (0,)), ((), ())), preferred_element_type=F32)


def mm_t(lhs, rhs):
    return lax.dot_general(lhs, rhs, (((1,), (1,)), ((), ())), preferred_element_type=F32)


def along_y(halves, right_ref):
    out = []
    for py in range(2):
        hi, lo = split(halves[py])
        full = mm(jnp.concatenate([hi, lo], 1), right_ref[py])
        out.append(full[:, :HALF] + full[:, HALF:])
    return out


def along_x(halves, left_ref):
    out = []
    for px in range(2):
        hi, lo = split(halves[px])
        full = mm(left_ref[px], jnp.concatenate([hi, lo], 0))
        out.append(full[:HALF] + full[HALF:])
    return out


def potentials(own, partners, right_ref, left_ref, coulomb_ref):
    states = []
    for partner in partners:
        density = own * partner
        even = density[:, :HALF] + density[:, HALF:]
        odd = density[:, :HALF] - density[:, HALF:]
        states.append(
            [jnp.concatenate([h[:HALF] + h[HALF:], h[:HALF] - h[HALF:]], 0) for h in (even, odd)]
        )
    states = [along_y(s, right_ref) for s in states]
    states = [
        [jnp.concatenate([s[0][px * HALF : (px + 1) * HALF], s[1][px * HALF : (px + 1) * HALF]], 1) for px in range(2)]
        for s in states
    ]
    states = [along_x(s, left_ref) for s in states]
    states = [[s[px] * coulomb_ref[px * HALF : (px + 1) * HALF] for px in range(2)] for s in states]
    states = [along_x(s, left_ref) for s in states]
    states = [
        [jnp.concatenate([s[0][:, py * HALF : (py + 1) * HALF], s[1][:, py * HALF : (py + 1) * HALF]], 0) for py in range(2)]
        for s in states
    ]
    states = [along_y(s, right_ref) for s in states]
    results = []
    for even, odd in states:
        both = jnp.concatenate([even + odd, even - odd], 1)
        results.append(jnp.concatenate([both[:HALF] + both[HALF:], both[:HALF] - both[HALF:]], 0))
    return results


STEPS = (
    (0, 0), (1, 0), (3, 0), (2, 0),
    (1, 1), (3, 1), (2, 1),
    (1, 3), (3, 3), (2, 3),
    (2, 2), (1, 2), (3, 2),
    (0, 1), (0, 3), (0, 2),
)


def pick(step, table):
    value = jnp.int32(table[0])
    for position, entry in enumerate(table):
        if position and entry != table[0]:
            value = jnp.where(step == position, jnp.int32(entry), value)
    return value


def kernel(
    coef_ref, list_ref, hart_x_ref, hart_y_ref, right_ref, left_ref, coulomb_ref, place_x_ref, place_y_ref,
    out_ref,
    send_ref, got_ref, grids, fields, others,
    s_chunk, r_chunk, s_near, r_near, s_far, r_far, s_sib, r_sib, s_field, r_field,
):
    band = lax.axis_index("band")
    plane = lax.axis_index("plane")
    n_band = lax.axis_size("band")
    y = plane // 2
    core = plane % 2

    def at_plane(dy, flip):
        return (band, (y + dy) % 4 * 2 + (core + flip) % 2)

    def at_band(t):
        return ((band + t + n_band) % n_band, plane)

    barrier = pltpu.get_barrier_semaphore()
    peers = [at_plane(dy, flip) for dy in range(4) for flip in range(2) if (dy, flip) != (0, 0)]
    peers += [at_band(t) for t in (1, 2, 3, -1, -2, -3)]
    for peer in peers:
        pl.semaphore_signal(barrier, inc=1, device_id=peer, device_id_type=MESH)

    lane = lax.broadcasted_iota(jnp.int32, (CHUNK, HALF), 1)
    row = lax.broadcasted_iota(jnp.int32, (CHUNK, HALF), 0)
    listed = jnp.broadcast_to(list_ref[...].astype(F32), (CHUNK, HALF))
    column = jnp.sum(jnp.where(lane == row, listed, 0.0), axis=1, keepdims=True)
    tag = jnp.broadcast_to(column, (CHUNK, HALF))
    tail = jnp.where(lane == N - HALF, tag, 0.0)
    for b in range(BANDS):
        chunk = coef_ref[:, b * N : (b + 1) * N]
        send_ref[b, :SLOTS, :N] = chunk
        send_ref[b, :SLOTS, N:] = tail[:SLOTS, N - HALF :]
        send_ref[b, SLOTS:, :] = jnp.zeros((CHUNK - SLOTS, FULL), F32)
        send_ref[b, SLOTS:, N:] = tail[SLOTS:, N - HALF :]
    for g in range(11):
        grids[g, ROWS:, :] = jnp.zeros((FULL - ROWS, FULL), F32)
    pl.semaphore_wait(barrier, len(peers))

    chunk_copies = {}
    for dy in (2, 1, 3, 0):
        for flip in range(2):
            if (dy, flip) == (0, 0):
                continue
            slot = dy * 2 + flip
            target = at_plane(dy, flip)
            copy = pltpu.make_async_remote_copy(
                src_ref=send_ref.at[target[1]], dst_ref=got_ref.at[slot],
                send_sem=s_chunk.at[slot], recv_sem=r_chunk.at[slot],
                device_id=target, device_id_type=MESH,
            )
            copy.start()
            chunk_copies[slot] = copy
    got_ref[0] = send_ref[plane]

    grid_lane = lax.broadcasted_iota(jnp.int32, (HALF, FULL), 1).astype(F32)
    phi = jnp.zeros((FULL, FULL), F32)
    for dy in (0, 1, 3, 2):
        for flip in range(2):
            if (dy, flip) != (0, 0):
                chunk_copies[dy * 2 + flip].wait_recv()
        rows = jnp.concatenate([got_ref[dy * 2], got_ref[dy * 2 + 1]], 0)
        hi, lo = split(rows)
        twice = mm_t(hart_x_ref[...], hi)
        columns = twice[:FULL] + twice[FULL:] + mm_t(hart_x_ref[:FULL], lo)
        picked = (jnp.broadcast_to(rows[:, N : N + 1], (HALF, FULL)) == grid_lane).astype(BF16)
        table = mm(picked, hart_y_ref[...]).astype(BF16)
        hi, lo = split(columns)
        phi += mm(hi, table[:, :FULL]) + mm(lo, table[:, :FULL]) + mm(hi, table[:, FULL:])
    grids[0] = phi

    def live(g):
        return grids.at[g, :ROWS]

    def grid_copy(target, src, dst, send, recv):
        return pltpu.make_async_remote_copy(
            src_ref=live(src), dst_ref=live(dst), send_sem=send, recv_sem=recv,
            device_id=target, device_id_type=MESH,
        )

    near = {dy: grid_copy(at_plane(dy, 0), 0, dy, s_near.at[dy], r_near.at[dy]) for dy in (1, 3, 2)}
    far = {t: grid_copy(at_band(t), 0, 3 + t, s_far.at[t], r_far.at[t]) for t in (1, 3, 2)}
    sib = {t: grid_copy(at_plane(0, 1), 0 if t == 0 else 3 + t, 7 + t, s_sib.at[t], r_sib.at[t]) for t in range(4)}
    sib[0].start()
    for k in (1, 3, 2):
        near[k].start()
        far[k].start()

    field_copies = {
        dy: pltpu.make_async_remote_copy(
            src_ref=fields.at[dy, :ROWS], dst_ref=others.at[dy - 1, :ROWS],
            send_sem=s_field.at[dy], recv_sem=r_field.at[dy],
            device_id=at_plane(4 - dy, 0), device_id_type=MESH,
        )
        for dy in (1, 2, 3)
    }

    for n in range(4):
        fields[n] = jnp.zeros((FULL, FULL), F32)

    def before(step):
        if step == 0:
            sib[0].wait_recv()
        if step == 1:
            near[1].wait_recv()
        if step == 2:
            near[3].wait_recv()
            far[1].wait_recv()
            sib[1].start()
        if step == 3:
            near[2].wait_recv()
            far[3].wait_recv()
            sib[3].start()
        if step == 4:
            sib[1].wait_recv()
        if step == 6:
            far[2].wait_recv()
            sib[2].start()
        if step == 7:
            sib[3].wait_recv()
        if step == 10:
            sib[2].wait_recv()

    def after(step):
        if step == 10:
            field_copies[2].start()
        if step == 11:
            field_copies[1].start()
        if step == 12:
            field_copies[3].start()

    def body(step, carry):
        for k in (0, 1, 2, 3, 4, 6, 7, 10):
            pl.when(step == k)(functools.partial(before, k))
        n = pick(step, [s[0] for s in STEPS])
        t = pick(step, [s[1] for s in STEPS])
        first = jnp.where(t == 0, 0, 3 + t)
        own = grids[n]
        partners = [grids[first], grids[7 + t]]
        values = potentials(own, partners, right_ref, left_ref, coulomb_ref)
        fields[n] += values[0] * partners[0] + values[1] * partners[1]
        for k in (10, 11, 12):
            pl.when(step == k)(functools.partial(after, k))
        return carry

    lax.fori_loop(0, len(STEPS), body, 0)

    for dy in (1, 2, 3):
        field_copies[dy].wait_recv()
    total = fields[0, :ROWS] + others[0, :ROWS] + others[1, :ROWS] + others[2, :ROWS]
    total = jnp.concatenate([total, jnp.zeros((FULL - ROWS, FULL), F32)], 0)
    hi, lo = split(total)
    ordered = mm(hi, place_y_ref[...]) + mm(lo, place_y_ref[...])
    hi, lo = split(ordered)
    ordered = mm(place_x_ref[...], hi) + mm(place_x_ref[...], lo)
    out_ref[0] = ordered[:, :N]

    for copy in (*chunk_copies.values(), *near.values(), *far.values(), *sib.values(), *field_copies.values()):
        copy.wait_send()


def on_device(stick_coef, stick_list):
    tables = [jnp.asarray(t) for t in make_tables()]
    dma = pltpu.SemaphoreType.DMA
    padded = jnp.full((1, HALF), -1, jnp.int32).at[0, :SLOTS].set(stick_list)
    return pl.pallas_call(
        kernel,
        out_shape=jax.ShapeDtypeStruct((1, N, N), F32),
        in_specs=[pl.BlockSpec(memory_space=pltpu.VMEM)] * 9,
        out_specs=pl.BlockSpec(memory_space=pltpu.VMEM),
        scratch_shapes=[
            pltpu.VMEM((BANDS, CHUNK, FULL), F32),
            pltpu.VMEM((BANDS, CHUNK, FULL), F32),
            pltpu.VMEM((11, FULL, FULL), F32),
            pltpu.VMEM((4, FULL, FULL), F32),
            pltpu.VMEM((3, FULL, FULL), F32),
            dma((8,)), dma((8,)), dma((4,)), dma((4,)), dma((4,)), dma((4,)),
            dma((4,)), dma((4,)), dma((4,)), dma((4,)),
        ],
        compiler_params=pltpu.CompilerParams(
            collective_id=0, has_side_effects=True, vmem_limit_bytes=48 * 1024 * 1024
        ),
    )(stick_coef, padded, *tables)


def solution(mesh):
    in_specs = (P("plane", "band"), P("plane"))
    out_specs = P(("band", "plane"), None, None)
    return jax.shard_map(on_device, mesh=mesh, in_specs=in_specs, out_specs=out_specs, check_vma=False)
```

```python
import functools
import math

import jax
import jax.numpy as jnp
import ml_dtypes
import numpy as np
from jax import lax
from jax.experimental import pallas as pl
from jax.experimental.pallas import tpu as pltpu
from jax.sharding import PartitionSpec as P

N = 240
HALF = 128
FULL = 256
ROWS = 248
SLOTS = 60
CHUNK = 64
BANDS = 8
MESH = pl.DeviceIdType.MESH
F32 = jnp.float32
BF16 = jnp.bfloat16


def split_np(values):
    high = values.astype(np.float32).astype(ml_dtypes.bfloat16)
    low = (values - high.astype(np.float64)).astype(np.float32).astype(ml_dtypes.bfloat16)
    return high, low


def make_tables():
    spot = -np.ones(FULL, np.int64)
    spot[:121] = np.arange(121)
    spot[HALF + 1 : HALF + 120] = N - np.arange(1, 120)
    index = np.arange(N)
    phase = (index[:, None] * index[None, :] % N) * (2.0 * np.pi / N)
    hart = (np.cos(phase) + np.sin(phase)) / math.sqrt(N)
    folded = np.zeros((FULL, FULL))
    folded[spot >= 0, :N] = hart[spot[spot >= 0]]
    f_hi, f_lo = split_np(folded)
    cosine = np.zeros((HALF, HALF))
    cosine[:121, :121] = np.cos(phase[:121, :121]) / math.sqrt(N)
    sine = np.zeros((HALF, HALF))
    sine[1:120, 1:120] = np.sin(phase[1:120, 1:120]) / math.sqrt(N)
    right, left = [], []
    for table in (cosine, sine):
        hi, lo = split_np(table)
        right.append(np.block([[hi, lo], [hi, lo]]))
        left.append(np.block([[hi, hi], [lo, lo]]))
    freq = np.arange(HALF).astype(np.float64)
    weight = np.where((freq == 0) | (freq == 120), 1.0, 2.0)
    squared = freq[:, None] ** 2 + freq[None, :] ** 2
    coulomb = np.where(squared > 0, 0.25 * N / np.maximum(squared, 1.0), 0.0)
    coulomb = coulomb * weight[:, None] * weight[None, :]
    even = (freq <= 120).astype(np.float64)
    odd = ((freq >= 1) & (freq <= 119)).astype(np.float64)
    live = np.concatenate([even, odd])
    coulomb = (np.tile(coulomb, (2, 2)) * live[:, None] * live[None, :]).astype(np.float32)
    place = np.zeros((FULL, FULL), np.float32)
    for p in range(FULL):
        if spot[p] >= 0:
            place[p, spot[p]] = 1.0
    bf16 = ml_dtypes.bfloat16
    blocks = [f_hi.T, f_lo.T, f_hi, f_lo, *right, *left, place.astype(bf16), place.T.astype(bf16)]
    return np.concatenate(blocks, 0), coulomb


def split(values):
    high = values.astype(BF16)
    low = (values - high.astype(F32)).astype(BF16)
    return high, low


def mm(lhs, rhs):
    return lax.dot_general(lhs, rhs, (((1,), (0,)), ((), ())), preferred_element_type=F32)


def mm_t(lhs, rhs):
    return lax.dot_general(lhs, rhs, (((1,), (1,)), ((), ())), preferred_element_type=F32)


def along_lanes(halves, tables):
    out = []
    for p in range(2):
        hi, lo = split(halves[p])
        full = mm(jnp.concatenate([hi, lo], 1), tables[RIGHT + p])
        out.append(full[:, :HALF] + full[:, HALF:])
    return out


def along_rows(halves, tables):
    out = []
    for p in range(2):
        hi, lo = split(halves[p])
        full = mm(tables[LEFT + p], jnp.concatenate([hi, lo], 0))
        out.append(full[:HALF] + full[HALF:])
    return out


def to_rows(pair):
    return [jnp.concatenate([pair[0][k * HALF : (k + 1) * HALF], pair[1][k * HALF : (k + 1) * HALF]], 1) for k in range(2)]


def to_lanes(pair):
    return [jnp.concatenate([pair[0][:, k * HALF : (k + 1) * HALF], pair[1][:, k * HALF : (k + 1) * HALF]], 0) for k in range(2)]


def fold_rows(values):
    return jnp.concatenate([values[:HALF] + values[HALF:], values[:HALF] - values[HALF:]], 0)


def potentials(own, partners, tables, coulomb_ref):
    states = []
    for partner in partners:
        plus, minus = own[0] * partner[0], own[1] * partner[1]
        states.append([fold_rows(plus + minus), fold_rows(plus - minus)])
    states = [to_rows(along_lanes(s, tables)) for s in states]
    states = [along_rows(s, tables) for s in states]
    states = [[s[k] * coulomb_ref[k * HALF : (k + 1) * HALF] for k in range(2)] for s in states]
    states = [to_lanes(along_rows(s, tables)) for s in states]
    states = [along_lanes(s, tables) for s in states]
    return [[fold_rows(even + odd), fold_rows(even - odd)] for even, odd in states]


BACK_HI, BACK_LO, HART_HI, HART_LO, RIGHT, LEFT, PLACE, PLACE_T = 0, 1, 2, 3, 4, 6, 8, 9
TAG = 121
NEAR, FAR, SIB, VIA = 0, 3, 7, 11

STEPS = (
    (0, 0), (1, 0), (3, 0),
    (1, 3), (3, 3), (1, 1), (3, 1),
    (2, 0), (2, 3), (2, 1), (2, 2), (1, 2), (3, 2),
    (0, 3), (0, 1), (0, 2),
)


def pick(step, table):
    value = jnp.int32(table[0])
    for position, entry in enumerate(table):
        if position and entry != table[0]:
            value = jnp.where(step == position, jnp.int32(entry), value)
    return value


def kernel(
    coef_hbm, list_hbm, table_hbm, coulomb_hbm, out_ref,
    coef_ref, list_ref, tables, coulomb_ref, send_ref, got_ref, stick_ref, grids, fields, others, passing,
    local_sem, send_sem, recv_sem,
):
    band = lax.axis_index("band")
    plane = lax.axis_index("plane")
    n_band = lax.axis_size("band")
    y, core = plane // 2, plane % 2
    z, x = band // 4, band % 4
    n_z = n_band // 4
    is_head, is_wrap = x == 0, x == 3

    def at_plane(dy, flip):
        return (band, (y + dy) % 4 * 2 + (core + flip) % 2)

    def at_band(t):
        return ((band + t + n_band) % n_band, plane)

    def at_chip(dz, dx):
        return ((z + dz + n_z) % n_z * 4 + (x + dx + 4) % 4, plane)

    next_target = (jnp.where(is_wrap, at_chip(0, 1)[0], at_band(1)[0]), plane)

    barrier = pltpu.get_barrier_semaphore()
    peers = [at_plane(dy, flip) for dy in range(4) for flip in range(2) if (dy, flip) != (0, 0)]
    peers += [at_band(t) for t in (1, 3, -1, -3)]
    peers += [at_chip(0, 1), at_chip(0, -1), at_chip(1, 0), at_chip(-1, 0)]
    for peer in peers:
        pl.semaphore_signal(barrier, inc=1, device_id=peer, device_id_type=MESH)

    loads = [
        pltpu.make_async_copy(list_hbm, list_ref, local_sem.at[0]),
        pltpu.make_async_copy(coef_hbm, coef_ref, local_sem.at[1]),
        pltpu.make_async_copy(table_hbm.at[:4], tables.at[:4], local_sem.at[2]),
        pltpu.make_async_copy(table_hbm.at[4:], tables.at[4:], local_sem.at[3]),
        pltpu.make_async_copy(coulomb_hbm, coulomb_ref, local_sem.at[4]),
    ]
    for load in loads:
        load.start()
    for g in range(VIA + 1):
        for h in range(2):
            grids[g, h, ROWS:, :] = jnp.zeros((FULL - ROWS, HALF), F32)

    lane = lax.broadcasted_iota(jnp.int32, (CHUNK, HALF), 1)
    row = lax.broadcasted_iota(jnp.int32, (CHUNK, HALF), 0)
    loads[0].wait()
    listed = jnp.concatenate([list_ref[...].astype(F32), jnp.full((1, HALF - SLOTS), -1.0, F32)], 1)
    column = jnp.sum(jnp.where(lane == row, jnp.broadcast_to(listed, (CHUNK, HALF)), 0.0), axis=1, keepdims=True)
    tag = jnp.broadcast_to(column, (CHUNK, HALF))
    loads[1].wait()
    loads[2].wait()
    for b in range(BANDS):
        chunk = jnp.concatenate([coef_ref[:, b * N : (b + 1) * N], jnp.zeros((SLOTS, FULL - N), F32)], 1)
        chunk = jnp.concatenate([chunk, jnp.zeros((CHUNK - SLOTS, FULL), F32)], 0)
        hi, lo = split(chunk)
        moved = mm(jnp.concatenate([hi, lo], 0), tables[BACK_HI])
        moved = moved[:CHUNK] + moved[CHUNK:] + mm(hi, tables[BACK_LO])
        send_ref[b, 0] = jnp.where(lane == TAG, tag, moved[:, :HALF])
        send_ref[b, 1] = moved[:, HALF:]
    pl.semaphore_wait(barrier, len(peers))

    count = [0]
    copies = []

    def across(src, dst, send, recv, target):
        return pltpu.make_async_remote_copy(
            src_ref=src, dst_ref=dst, send_sem=send_sem.at[send], recv_sem=recv_sem.at[recv],
            device_id=target, device_id_type=MESH,
        )

    def plain(src, dst, target):
        copies.append(across(src, dst, count[0], count[0], target))
        count[0] += 1
        return copies[-1]

    chunk_copies = {}
    for h in range(2):
        for dy in (2, 1, 3, 0):
            for flip in range(2):
                if (dy, flip) != (0, 0):
                    target = at_plane(dy, flip)
                    slot = dy * 2 + flip
                    chunk_copies[slot, h] = plain(send_ref.at[target[1], h], got_ref.at[slot, h], target)
                    chunk_copies[slot, h].start()
    got_ref[0] = send_ref[plane]

    def live(g, h):
        return grids.at[g, h, :ROWS]

    def move(target, src, dst):
        return [plain(live(src, h), live(dst, h), target) for h in range(2)]

    near = {1: move(at_plane(1, 0), 0, NEAR + 1), 3: move(at_plane(3, 0), 0, NEAR + 3)}
    near[2] = [
        plain(live(NEAR + 1, 0), live(NEAR + 2, 0), at_plane(1, 0)),
        plain(live(NEAR + 3, 1), live(NEAR + 2, 1), at_plane(3, 0)),
    ]
    far = {3: move(at_band(3), 0, FAR + 3)}
    relay_at, via_at, far_at = count[0], count[0] + 2, count[0] + 4
    count[0] += 6

    relay = [across(live(VIA, h), live(FAR + 1, h), relay_at + h, far_at + h, at_chip(1, 0)) for h in range(2)]
    relayed = [across(live(VIA, h), live(VIA, h), via_at + h, via_at + h, at_chip(0, 1)) for h in range(2)]
    onward = [
        across(live(0, h), live(jnp.where(is_wrap, VIA, FAR + 1), h), far_at + h, jnp.where(is_wrap, via_at, far_at) + h, next_target)
        for h in range(2)
    ]
    far[1] = [across(live(0, h), live(FAR + 1, h), far_at + h, far_at + h, at_band(1)) for h in range(2)]
    far[2] = [
        plain(live(FAR + 1, 0), live(FAR + 2, 0), at_band(1)),
        plain(live(FAR + 3, 1), live(FAR + 2, 1), at_band(-1)),
    ]
    sib = {t: move(at_plane(0, 1), 0 if t == 0 else FAR + t, SIB + t) for t in range(4)}

    stick_lane = lax.broadcasted_iota(jnp.int32, (HALF, FULL), 1).astype(F32)
    lane = lax.broadcasted_iota(jnp.int32, (FULL, HALF), 1)
    for h in range(2):
        phi = jnp.zeros((FULL, HALF), F32)
        for position, dy in enumerate((0, 1, 3, 2)):
            for flip in range(2):
                if (dy, flip) != (0, 0):
                    chunk_copies[dy * 2 + flip, h].wait_recv()
            rows = jnp.concatenate([got_ref[dy * 2, h], got_ref[dy * 2 + 1, h]], 0)
            if h == 0:
                picked = (jnp.broadcast_to(rows[:, TAG : TAG + 1], (HALF, FULL)) == stick_lane).astype(BF16)
                hart = jnp.concatenate([tables[HART_HI], tables[HART_LO]], 0)
                stick_ref[position] = mm_t(hart, picked).astype(BF16)
            hi, lo = split(rows)
            full = mm(stick_ref[position], jnp.concatenate([hi, lo], 1))
            full = full[:FULL] + full[FULL:]
            phi += full[:, :HALF] + full[:, HALF:]
        if h == 0:
            phi = jnp.where(lane < TAG, phi, 0.0)
        grids[0, h] = phi
        near[1][h].start()
        onward[h].start()
        near[3][h].start()
        far[3][h].start()
        sib[0][h].start()

    back = {
        1: [plain(fields.at[1, h, :ROWS], others.at[0, h, :ROWS], at_plane(3, 0)) for h in range(2)],
        3: [plain(fields.at[3, h, :ROWS], others.at[1, h, :ROWS], at_plane(1, 0)) for h in range(2)],
        2: [
            plain(fields.at[2, 0, :ROWS], passing.at[0, :ROWS], at_plane(3, 0)),
            plain(fields.at[2, 1, :ROWS], passing.at[1, :ROWS], at_plane(1, 0)),
        ],
    }

    for n in range(4):
        fields[n] = jnp.zeros((2, FULL, HALF), F32)
    loads[3].wait()
    loads[4].wait()

    def received(pair):
        pair[0].wait_recv()
        pair[1].wait_recv()

    def started(pair):
        pair[0].start()
        pair[1].start()

    def pass_on(h):
        relayed[h].wait_recv()
        relay[h].start()

    def before_0():
        received(sib[0])

    def before_1():
        near[1][0].wait_recv()
        near[2][0].start()
        pl.when(is_head)(functools.partial(pass_on, 0))
        near[3][1].wait_recv()
        near[2][1].start()
        far[3][1].wait_recv()
        far[2][1].start()
        pl.when(is_head)(functools.partial(pass_on, 1))
        near[1][1].wait_recv()

    def before_2():
        near[3][0].wait_recv()
        far[1][0].wait_recv()
        far[2][0].start()
        far[3][0].wait_recv()
        started(sib[3])

    def before_3():
        received(sib[3])

    def before_4():
        far[1][1].wait_recv()
        started(sib[1])

    def before_5():
        received(sib[1])

    def before_7():
        received(near[2])

    def before_8():
        received(far[2])
        started(sib[2])

    def before_10():
        received(sib[2])

    def after_10():
        started(back[2])

    def after_11():
        back[1][1].start()

    def after_12():
        back[3][0].start()

    def after_14():
        back[2][0].wait_recv()
        fields[1, 0, :ROWS] += passing[0, :ROWS]
        back[1][0].start()
        back[2][1].wait_recv()
        fields[3, 1, :ROWS] += passing[1, :ROWS]
        back[3][1].start()

    before = {0: before_0, 1: before_1, 2: before_2, 3: before_3, 4: before_4, 5: before_5, 7: before_7, 8: before_8, 10: before_10}
    after = {10: after_10, 11: after_11, 12: after_12, 14: after_14}

    def body(step, carry):
        for k, action in before.items():
            pl.when(step == k)(action)
        n = pick(step, [s[0] for s in STEPS])
        t = pick(step, [s[1] for s in STEPS])
        first = jnp.where(t == 0, 0, FAR + t)
        own = [grids[n, h] for h in range(2)]
        partners = [[grids[g, h] for h in range(2)] for g in (first, SIB + t)]
        values = potentials(own, partners, tables, coulomb_ref)
        for h in range(2):
            fields[n, h] += values[0][h] * partners[0][h] + values[1][h] * partners[1][h]
        for k, action in after.items():
            pl.when(step == k)(action)
        return carry

    lax.fori_loop(0, len(STEPS), body, 0)

    received(back[1])
    received(back[3])
    halves = []
    for h in range(2):
        half = fields[0, h, :ROWS] + others[0, h, :ROWS] + others[1, h, :ROWS]
        halves.append(jnp.concatenate([half, jnp.zeros((FULL - ROWS, HALF), F32)], 0))
    hi, lo = split(jnp.concatenate(halves, 1))
    ordered = mm_t(tables[PLACE_T], hi) + mm_t(tables[PLACE_T], lo)
    hi, lo = split(ordered)
    ordered = mm(hi, tables[PLACE]) + mm(lo, tables[PLACE])
    out_ref[0] = ordered[:N, :N]

    def sent(pair):
        pair[0].wait_send()
        pair[1].wait_send()

    sent(onward)
    pl.when(is_head)(functools.partial(sent, relay))
    for copy in copies:
        copy.wait_send()


def on_device(stick_coef, stick_list):
    tables, coulomb = make_tables()
    tables = jnp.asarray(tables.reshape(10, FULL, FULL))
    dma = pltpu.SemaphoreType.DMA
    return pl.pallas_call(
        kernel,
        out_shape=jax.ShapeDtypeStruct((1, N, N), F32),
        in_specs=[pl.BlockSpec(memory_space=pltpu.HBM)] * 4,
        out_specs=pl.BlockSpec(memory_space=pltpu.VMEM),
        scratch_shapes=[
            pltpu.VMEM((SLOTS, BANDS * N), F32),
            pltpu.VMEM((1, SLOTS), jnp.int32),
            pltpu.VMEM((10, FULL, FULL), BF16),
            pltpu.VMEM((FULL, FULL), F32),
            pltpu.VMEM((BANDS, 2, CHUNK, HALF), F32),
            pltpu.VMEM((BANDS, 2, CHUNK, HALF), F32),
            pltpu.VMEM((4, 2 * FULL, HALF), BF16),
            pltpu.VMEM((VIA + 1, 2, FULL, HALF), F32),
            pltpu.VMEM((4, 2, FULL, HALF), F32),
            pltpu.VMEM((2, 2, FULL, HALF), F32),
            pltpu.VMEM((2, FULL, HALF), F32),
            dma((5,)),
            dma((64,)),
            dma((64,)),
        ],
        compiler_params=pltpu.CompilerParams(
            collective_id=0, has_side_effects=True, vmem_limit_bytes=60 * 1024 * 1024
        ),
    )(stick_coef, stick_list.reshape(1, SLOTS), tables, jnp.asarray(coulomb))


def solution(mesh):
    in_specs = (P("plane", "band"), P("plane"))
    out_specs = P(("band", "plane"), None, None)
    return jax.shard_map(on_device, mesh=mesh, in_specs=in_specs, out_specs=out_specs, check_vma=False)
```

```python
import functools
import math

import jax
import jax.numpy as jnp
import ml_dtypes
import numpy as np
from jax import lax
from jax.experimental import pallas as pl
from jax.experimental.pallas import tpu as pltpu
from jax.sharding import PartitionSpec as P

N = 240
HALF = 128
FULL = 256
ROWS = 248
SLOTS = 60
CHUNK = 64
BANDS = 8
MESH = pl.DeviceIdType.MESH
F32 = jnp.float32
BF16 = jnp.bfloat16


def split_np(values):
    high = values.astype(np.float32).astype(ml_dtypes.bfloat16)
    low = (values - high.astype(np.float64)).astype(np.float32).astype(ml_dtypes.bfloat16)
    return high, low


def make_tables():
    spot = -np.ones(FULL, np.int64)
    spot[:121] = np.arange(121)
    spot[HALF + 1 : HALF + 120] = N - np.arange(1, 120)
    index = np.arange(N)
    phase = (index[:, None] * index[None, :] % N) * (2.0 * np.pi / N)
    hart = (np.cos(phase) + np.sin(phase)) / math.sqrt(N)
    folded = np.zeros((FULL, FULL))
    folded[spot >= 0, :N] = hart[spot[spot >= 0]]
    f_hi, f_lo = split_np(folded)
    cosine = np.zeros((HALF, HALF))
    cosine[:121, :121] = np.cos(phase[:121, :121]) / math.sqrt(N)
    sine = np.zeros((HALF, HALF))
    sine[1:120, 1:120] = np.sin(phase[1:120, 1:120]) / math.sqrt(N)
    right, left = [], []
    for table in (cosine, sine):
        hi, lo = split_np(table)
        right.append(np.block([[hi, lo], [hi, lo]]))
        left.append(np.block([[hi, hi], [lo, lo]]))
    freq = np.arange(HALF).astype(np.float64)
    weight = np.where((freq == 0) | (freq == 120), 1.0, 2.0)
    squared = freq[:, None] ** 2 + freq[None, :] ** 2
    coulomb = np.where(squared > 0, 0.25 * N / np.maximum(squared, 1.0), 0.0)
    coulomb = coulomb * weight[:, None] * weight[None, :]
    even = (freq <= 120).astype(np.float64)
    odd = ((freq >= 1) & (freq <= 119)).astype(np.float64)
    live = np.concatenate([even, odd])
    coulomb = (np.tile(coulomb, (2, 2)) * live[:, None] * live[None, :]).astype(np.float32)
    place = np.zeros((FULL, FULL), np.float32)
    for p in range(FULL):
        if spot[p] >= 0:
            place[p, spot[p]] = 1.0
    bf16 = ml_dtypes.bfloat16
    blocks = [f_hi.T, f_lo.T, f_hi, f_lo, *right, *left, place.astype(bf16), place.T.astype(bf16)]
    return np.concatenate(blocks, 0), coulomb


def split(values):
    high = values.astype(BF16)
    low = (values - high.astype(F32)).astype(BF16)
    return high, low


def mm(lhs, rhs):
    return lax.dot_general(lhs, rhs, (((1,), (0,)), ((), ())), preferred_element_type=F32)


def mm_t(lhs, rhs):
    return lax.dot_general(lhs, rhs, (((1,), (1,)), ((), ())), preferred_element_type=F32)


def along_lanes(halves, tables):
    out = []
    for p in range(2):
        hi, lo = split(halves[p])
        full = mm(jnp.concatenate([hi, lo], 1), tables[RIGHT + p])
        out.append(full[:, :HALF] + full[:, HALF:])
    return out


def along_rows(halves, tables):
    out = []
    for p in range(2):
        hi, lo = split(halves[p])
        full = mm(tables[LEFT + p], jnp.concatenate([hi, lo], 0))
        out.append(full[:HALF] + full[HALF:])
    return out


def to_rows(pair):
    return [jnp.concatenate([pair[0][k * HALF : (k + 1) * HALF], pair[1][k * HALF : (k + 1) * HALF]], 1) for k in range(2)]


def to_lanes(pair):
    return [jnp.concatenate([pair[0][:, k * HALF : (k + 1) * HALF], pair[1][:, k * HALF : (k + 1) * HALF]], 0) for k in range(2)]


def fold_rows(values):
    return jnp.concatenate([values[:HALF] + values[HALF:], values[:HALF] - values[HALF:]], 0)


def potentials(pairs, tables, coulomb_ref):
    states = []
    for own, partner in pairs:
        plus, minus = own[0] * partner[0], own[1] * partner[1]
        states.append([fold_rows(plus + minus), fold_rows(plus - minus)])
    states = [to_rows(along_lanes(s, tables)) for s in states]
    states = [along_rows(s, tables) for s in states]
    states = [[s[k] * coulomb_ref[k * HALF : (k + 1) * HALF] for k in range(2)] for s in states]
    states = [to_lanes(along_rows(s, tables)) for s in states]
    states = [along_lanes(s, tables) for s in states]
    return [[fold_rows(even + odd), fold_rows(even - odd)] for even, odd in states]


BACK_HI, BACK_LO, HART_HI, HART_LO, RIGHT, LEFT, PLACE, PLACE_T = 0, 1, 2, 3, 4, 6, 8, 9
TAG = 121
NEAR, FAR, SIB, VIA = 0, 3, 7, 11

STEPS = (
    ((1, 0), (3, 0)),
    ((1, 3), (3, 3)),
    ((2, 0), (2, 3)),
    ((1, 1), (3, 1)),
    ((2, 1), (2, 2)),
    ((1, 2), (3, 2)),
    ((0, 0), (0, 3)),
    ((0, 1), (0, 2)),
)


def pick(step, table):
    value = jnp.int32(table[0])
    for position, entry in enumerate(table):
        if position and entry != table[0]:
            value = jnp.where(step == position, jnp.int32(entry), value)
    return value


def kernel(
    coef_hbm, list_hbm, table_hbm, coulomb_hbm, out_ref,
    coef_ref, list_ref, tables, coulomb_ref, send_ref, got_ref, stick_ref, grids, fields, others,
    local_sem, send_sem, recv_sem,
):
    band = lax.axis_index("band")
    plane = lax.axis_index("plane")
    n_band = lax.axis_size("band")
    y, core = plane // 2, plane % 2
    z, x = band // 4, band % 4
    n_z = n_band // 4
    is_head, is_wrap = x == 0, x == 3

    def at_plane(dy, flip):
        return (band, (y + dy) % 4 * 2 + (core + flip) % 2)

    def at_band(t):
        return ((band + t + n_band) % n_band, plane)

    def at_chip(dz, dx):
        return ((z + dz + n_z) % n_z * 4 + (x + dx + 4) % 4, plane)

    next_target = (jnp.where(is_wrap, at_chip(0, 1)[0], at_band(1)[0]), plane)

    barrier = pltpu.get_barrier_semaphore()
    peers = [at_plane(dy, flip) for dy in range(4) for flip in range(2) if (dy, flip) != (0, 0)]
    peers += [at_band(t) for t in (1, 3, -1, -3)]
    peers += [at_chip(0, 1), at_chip(0, -1), at_chip(1, 0), at_chip(-1, 0), at_chip(1, 1), at_chip(-1, -1)]
    for peer in peers:
        pl.semaphore_signal(barrier, inc=1, device_id=peer, device_id_type=MESH)

    loads = [
        pltpu.make_async_copy(list_hbm, list_ref, local_sem.at[0]),
        pltpu.make_async_copy(coef_hbm, coef_ref, local_sem.at[1]),
        pltpu.make_async_copy(table_hbm.at[:4], tables.at[:4], local_sem.at[2]),
        pltpu.make_async_copy(table_hbm.at[4:], tables.at[4:], local_sem.at[3]),
        pltpu.make_async_copy(coulomb_hbm, coulomb_ref, local_sem.at[4]),
    ]
    for load in loads:
        load.start()
    for g in range(VIA + 1):
        for h in range(2):
            grids[g, h, ROWS:, :] = jnp.zeros((FULL - ROWS, HALF), F32)

    lane = lax.broadcasted_iota(jnp.int32, (CHUNK, HALF), 1)
    row = lax.broadcasted_iota(jnp.int32, (CHUNK, HALF), 0)
    loads[0].wait()
    listed = jnp.concatenate([list_ref[...].astype(F32), jnp.full((1, HALF - SLOTS), -1.0, F32)], 1)
    column = jnp.sum(jnp.where(lane == row, jnp.broadcast_to(listed, (CHUNK, HALF)), 0.0), axis=1, keepdims=True)
    tag = jnp.broadcast_to(column, (CHUNK, HALF))
    loads[1].wait()
    loads[2].wait()
    for b in range(BANDS):
        chunk = jnp.concatenate([coef_ref[:, b * N : (b + 1) * N], jnp.zeros((SLOTS, FULL - N), F32)], 1)
        chunk = jnp.concatenate([chunk, jnp.zeros((CHUNK - SLOTS, FULL), F32)], 0)
        hi, lo = split(chunk)
        moved = mm(jnp.concatenate([hi, lo], 0), tables[BACK_HI])
        moved = moved[:CHUNK] + moved[CHUNK:] + mm(hi, tables[BACK_LO])
        send_ref[b, 0] = jnp.where(lane == TAG, tag, moved[:, :HALF])
        send_ref[b, 1] = moved[:, HALF:]
    pl.semaphore_wait(barrier, len(peers))

    count = [0]
    copies = []

    def across(src, dst, send, recv, target):
        return pltpu.make_async_remote_copy(
            src_ref=src, dst_ref=dst, send_sem=send_sem.at[send], recv_sem=recv_sem.at[recv],
            device_id=target, device_id_type=MESH,
        )

    def plain(src, dst, target):
        copies.append(across(src, dst, count[0], count[0], target))
        count[0] += 1
        return copies[-1]

    chunk_copies = {}
    for h in range(2):
        for dy, flip in ((2, 0), (2, 1), (1, 0), (3, 0), (1, 1), (3, 1), (0, 1)):
            target = at_plane(dy, flip)
            slot = dy * 2 + flip
            args = (send_ref.at[target[1], h], got_ref.at[slot, h])
            chunk_copies[slot, h] = across(*args, count[0], count[0], target)
            count[0] += 1
            if h:
                chunk_copies[slot, 0].wait_send()
                copies.append(chunk_copies[slot, 1])
            chunk_copies[slot, h].start()
    got_ref[0] = send_ref[plane]

    def piece(ref, g, q):
        return ref.at[g, q // 2, pl.ds(q % 2 * HALF, ROWS - HALF if q % 2 else HALF)]

    def live(g, q):
        return piece(grids, g, q)

    def move(target, src, dst):
        return [plain(live(src, q), live(dst, q), target) for q in range(4)]

    near = {1: move(at_plane(1, 0), 0, NEAR + 1), 3: move(at_plane(3, 0), 0, NEAR + 3)}
    near[2] = [plain(live(NEAR + (3 if q % 2 else 1), q), live(NEAR + 2, q), at_plane(3 if q % 2 else 1, 0)) for q in range(4)]
    far = {3: move(at_band(3), 0, FAR + 3)}
    relay_at, via_at, far_at = count[0], count[0] + 4, count[0] + 8
    count[0] += 12
    relay = [across(live(VIA, q), live(FAR + 1, q), relay_at + q, far_at + q, at_chip(1, 0)) for q in range(2)]
    relayed = [across(live(VIA, q), live(VIA, q), via_at + q, via_at + q, at_chip(0, 1)) for q in range(2)]
    far[1] = [across(live(0, q), live(FAR + 1, q), far_at + q, far_at + q, at_band(1)) for q in range(4)]
    onward = [
        across(live(0, q), live(jnp.where(is_wrap, VIA, FAR + 1), q), far_at + q, jnp.where(is_wrap, via_at, far_at) + q, next_target)
        for q in range(2)
    ] + far[1][2:]
    skip_target = (jnp.where(is_head, at_chip(1, 1)[0], at_band(1)[0]), plane)
    from_lower = {
        0: plain(live(jnp.where(is_head, VIA, FAR + 1), 0), live(FAR + 2, 0), skip_target),
        2: across(live(FAR + 1, 2), live(FAR + 2, 2), count[0], count[0], at_band(1)),
    }
    from_upper = {2: across(live(FAR + 3, 2), live(FAR + 2, 2), count[0], count[0], at_band(-1))}
    count[0] += 1
    for q in (1, 3):
        from_upper[q] = plain(live(FAR + 3, q), live(FAR + 2, q), at_band(-1))
    far[2] = [(from_upper if q % 2 else from_lower)[q] for q in range(4)]
    sib = {
        t: [plain(grids.at[FAR + t if t else 0, h, :ROWS], grids.at[SIB + t, h, :ROWS], at_plane(0, 1)) for h in range(2)]
        for t in range(4)
    }

    stick_lane = lax.broadcasted_iota(jnp.int32, (HALF, FULL), 1).astype(F32)
    lane = lax.broadcasted_iota(jnp.int32, (FULL, HALF), 1)
    for h in range(2):
        phi = jnp.zeros((FULL, HALF), F32)
        for position, dy in enumerate((0, 1, 3, 2)):
            for flip in range(2):
                if (dy, flip) != (0, 0):
                    chunk_copies[dy * 2 + flip, h].wait_recv()
            rows = jnp.concatenate([got_ref[dy * 2, h], got_ref[dy * 2 + 1, h]], 0)
            if h == 0:
                picked = (jnp.broadcast_to(rows[:, TAG : TAG + 1], (HALF, FULL)) == stick_lane).astype(BF16)
                hart = jnp.concatenate([tables[HART_HI], tables[HART_LO]], 0)
                stick_ref[position] = mm_t(hart, picked).astype(BF16)
            hi, lo = split(rows)
            full = mm(stick_ref[position], jnp.concatenate([hi, lo], 1))
            full = full[:FULL] + full[FULL:]
            phi += full[:, :HALF] + full[:, HALF:]
        if h == 0:
            phi = jnp.where(lane < TAG, phi, 0.0)
        grids[0, h] = phi
        for first, second in ((2 * h, 2 * h + 1), (2 * h + 1, 2 * h)):
            near[1][first].start()
            onward[first].start()
            near[3][second].start()
            far[3][second].start()
        sib[0][h].start()

    back = {
        1: [plain(piece(fields, 1, q), piece(others, 0, q), at_plane(3, 0)) for q in range(4)],
        3: [plain(piece(fields, 3, q), piece(others, 1, q), at_plane(1, 0)) for q in range(4)],
        2: [plain(piece(fields, 2, q), piece(others, 2, q), at_plane(3 if q < 2 else 1, 0)) for q in range(4)],
    }

    for n in range(4):
        fields[n] = jnp.zeros((2, FULL, HALF), F32)
    loads[3].wait()
    loads[4].wait()

    def received(parts):
        for part in parts:
            part.wait_recv()

    def started(parts):
        for part in parts:
            part.start()

    def from_below(q):
        near[1][q].wait_recv()
        near[2][q].start()

        @pl.when(is_head)
        def _():
            if q == 0:
                relayed[0].wait_recv()
                relay[0].start()
                from_lower[0].start()

        @pl.when(jnp.logical_not(is_head))
        def _():
            far[1][q].wait_recv()
            from_lower[q].start()

    def from_above(q):
        near[3][q].wait_recv()
        near[2][q].start()
        far[3][q].wait_recv()
        from_upper[q].start()

        @pl.when(is_head)
        def _():
            if q == 1:
                relayed[1].wait_recv()
                relay[1].start()

        @pl.when(x == 2)
        def _():
            if q == 3:
                far[3][2].wait_recv()
                from_upper[2].start()

    def share(h):
        if h == 0:
            far[3][0].wait_recv()
        else:
            pl.when(x != 2)(far[3][2].wait_recv)
        sib[3][h].start()

        @pl.when(jnp.logical_not(is_head))
        def _():
            far[1][2 * h + 1].wait_recv()
            sib[1][h].start()

    def share_late(h):
        @pl.when(is_head)
        def _():
            received(far[1][2 * h : 2 * h + 2])
            sib[1][h].start()

        received(far[2][2 * h : 2 * h + 2])
        sib[2][h].start()

    def before_0():
        from_below(0)
        from_above(1)
        share(0)
        from_below(2)
        from_above(3)
        share(1)
        received((near[1][1], near[1][3], near[3][0], near[3][2]))
        received(sib[0])

    def before_1():
        received(sib[3])

    def before_2():
        share_late(0)
        received(near[2])

    def before_3():
        share_late(1)
        received(sib[1])

    def before_4():
        received(sib[2])

    def after_4():
        started(back[2])

    def after_5():
        started(back[1][2:])
        started(back[3][:2])

    def merge(n, q):
        back[2][q].wait_recv()
        piece(fields, n, q)[...] += piece(others, 2, q)[...]
        back[n][q].start()

    def after_7():
        for q in range(2):
            merge(1, q)
            merge(3, 2 + q)

    before = {0: before_0, 1: before_1, 2: before_2, 3: before_3, 4: before_4}
    after = {4: after_4, 5: after_5, 7: after_7}

    def body(step, carry):
        for k, action in before.items():
            pl.when(step == k)(action)
        pairs, places = [], []
        for part in range(2):
            n = pick(step, [s[part][0] for s in STEPS])
            t = pick(step, [s[part][1] for s in STEPS])
            own = [grids[n, h] for h in range(2)]
            for g in (jnp.where(t == 0, 0, FAR + t), SIB + t):
                pairs.append((own, [grids[g, h] for h in range(2)]))
            places.append(n)
        values = potentials(pairs, tables, coulomb_ref)
        for part, n in enumerate(places):
            for h in range(2):
                first, second = 2 * part, 2 * part + 1
                fields[n, h] += values[first][h] * pairs[first][1][h] + values[second][h] * pairs[second][1][h]
        for k, action in after.items():
            pl.when(step == k)(action)
        return carry

    lax.fori_loop(0, len(STEPS), body, 0)

    received(back[1])
    received(back[3])
    halves = []
    for h in range(2):
        half = fields[0, h, :ROWS] + others[0, h, :ROWS] + others[1, h, :ROWS]
        halves.append(jnp.concatenate([half, jnp.zeros((FULL - ROWS, HALF), F32)], 0))
    hi, lo = split(jnp.concatenate(halves, 1))
    ordered = mm_t(tables[PLACE_T], hi) + mm_t(tables[PLACE_T], lo)
    hi, lo = split(ordered)
    ordered = mm(hi, tables[PLACE]) + mm(lo, tables[PLACE])
    out_ref[0] = ordered[:N, :N]

    def sent(parts):
        for part in parts:
            part.wait_send()

    sent(onward)
    pl.when(is_head)(functools.partial(sent, relay))
    pl.when(jnp.logical_not(is_head))(from_lower[2].wait_send)
    pl.when(x == 2)(from_upper[2].wait_send)
    for copy in copies:
        copy.wait_send()


def on_device(stick_coef, stick_list):
    tables, coulomb = make_tables()
    tables = jnp.asarray(tables.reshape(10, FULL, FULL))
    dma = pltpu.SemaphoreType.DMA
    return pl.pallas_call(
        kernel,
        out_shape=jax.ShapeDtypeStruct((1, N, N), F32),
        in_specs=[pl.BlockSpec(memory_space=pltpu.HBM)] * 4,
        out_specs=pl.BlockSpec(memory_space=pltpu.VMEM),
        scratch_shapes=[
            pltpu.VMEM((SLOTS, BANDS * N), F32),
            pltpu.VMEM((1, SLOTS), jnp.int32),
            pltpu.VMEM((10, FULL, FULL), BF16),
            pltpu.VMEM((FULL, FULL), F32),
            pltpu.VMEM((BANDS, 2, CHUNK, HALF), F32),
            pltpu.VMEM((BANDS, 2, CHUNK, HALF), F32),
            pltpu.VMEM((4, 2 * FULL, HALF), BF16),
            pltpu.VMEM((VIA + 1, 2, FULL, HALF), F32),
            pltpu.VMEM((4, 2, FULL, HALF), F32),
            pltpu.VMEM((3, 2, FULL, HALF), F32),
            dma((5,)),
            dma((84,)),
            dma((84,)),
        ],
        compiler_params=pltpu.CompilerParams(
            collective_id=0, has_side_effects=True, vmem_limit_bytes=60 * 1024 * 1024
        ),
    )(stick_coef, stick_list.reshape(1, SLOTS), tables, jnp.asarray(coulomb))


def solution(mesh):
    in_specs = (P("plane", "band"), P("plane"))
    out_specs = P(("band", "plane"), None, None)
    return jax.shard_map(on_device, mesh=mesh, in_specs=in_specs, out_specs=out_specs, check_vma=False)
```

```python
import functools
import math

import jax
import jax.numpy as jnp
import ml_dtypes
import numpy as np
from jax import lax
from jax.experimental import pallas as pl
from jax.experimental.pallas import tpu as pltpu
from jax.sharding import PartitionSpec as P

N = 240
HALF = 128
FULL = 256
ROWS = 248
SLOTS = 60
CHUNK = 64
BANDS = 8
MESH = pl.DeviceIdType.MESH
F32 = jnp.float32
BF16 = jnp.bfloat16


def split_np(values):
    high = values.astype(np.float32).astype(ml_dtypes.bfloat16)
    low = (values - high.astype(np.float64)).astype(np.float32).astype(ml_dtypes.bfloat16)
    return high, low


def make_tables():
    spot = -np.ones(FULL, np.int64)
    spot[:121] = np.arange(121)
    spot[HALF + 1 : HALF + 120] = N - np.arange(1, 120)
    index = np.arange(N)
    phase = (index[:, None] * index[None, :] % N) * (2.0 * np.pi / N)
    hart = (np.cos(phase) + np.sin(phase)) / math.sqrt(N)
    folded = np.zeros((FULL, FULL))
    folded[spot >= 0, :N] = hart[spot[spot >= 0]]
    f_hi, f_lo = split_np(folded)
    cosine = np.zeros((HALF, HALF))
    cosine[:121, :121] = np.cos(phase[:121, :121]) / math.sqrt(N)
    sine = np.zeros((HALF, HALF))
    sine[1:120, 1:120] = np.sin(phase[1:120, 1:120]) / math.sqrt(N)
    right, left = [], []
    for table in (cosine, sine):
        hi, lo = split_np(table)
        right.append(np.block([[hi, lo], [hi, lo]]))
        left.append(np.block([[hi, hi], [lo, lo]]))
    freq = np.arange(HALF).astype(np.float64)
    weight = np.where((freq == 0) | (freq == 120), 1.0, 2.0)
    squared = freq[:, None] ** 2 + freq[None, :] ** 2
    coulomb = np.where(squared > 0, 0.25 * N / np.maximum(squared, 1.0), 0.0)
    coulomb = coulomb * weight[:, None] * weight[None, :]
    even = (freq <= 120).astype(np.float64)
    odd = ((freq >= 1) & (freq <= 119)).astype(np.float64)
    live = np.concatenate([even, odd])
    coulomb = (np.tile(coulomb, (2, 2)) * live[:, None] * live[None, :]).astype(np.float32)
    place = np.zeros((FULL, FULL), np.float32)
    for p in range(FULL):
        if spot[p] >= 0:
            place[p, spot[p]] = 1.0
    bf16 = ml_dtypes.bfloat16
    blocks = [f_hi.T, f_lo.T, f_hi, f_lo, *right, *left, place.astype(bf16), place.T.astype(bf16)]
    return np.concatenate(blocks, 0), coulomb


def split(values):
    high = values.astype(BF16)
    low = (values - high.astype(F32)).astype(BF16)
    return high, low


def mm(lhs, rhs):
    return lax.dot_general(lhs, rhs, (((1,), (0,)), ((), ())), preferred_element_type=F32)


def mm_t(lhs, rhs):
    return lax.dot_general(lhs, rhs, (((1,), (1,)), ((), ())), preferred_element_type=F32)


def along_lanes(halves, tables):
    out = []
    for p in range(2):
        hi, lo = split(halves[p])
        full = mm(jnp.concatenate([hi, lo], 1), tables[RIGHT + p])
        out.append(full[:, :HALF] + full[:, HALF:])
    return out


def along_rows(halves, tables):
    out = []
    for p in range(2):
        hi, lo = split(halves[p])
        full = mm(tables[LEFT + p], jnp.concatenate([hi, lo], 0))
        out.append(full[:HALF] + full[HALF:])
    return out


def to_rows(pair):
    return [jnp.concatenate([pair[0][k * HALF : (k + 1) * HALF], pair[1][k * HALF : (k + 1) * HALF]], 1) for k in range(2)]


def to_lanes(pair):
    return [jnp.concatenate([pair[0][:, k * HALF : (k + 1) * HALF], pair[1][:, k * HALF : (k + 1) * HALF]], 0) for k in range(2)]


def fold_rows(values):
    return jnp.concatenate([values[:HALF] + values[HALF:], values[:HALF] - values[HALF:]], 0)


def potentials(pairs, tables, coulomb_ref):
    states = []
    for own, partner in pairs:
        plus, minus = own[0] * partner[0], own[1] * partner[1]
        states.append([fold_rows(plus + minus), fold_rows(plus - minus)])
    states = [to_rows(along_lanes(s, tables)) for s in states]
    states = [along_rows(s, tables) for s in states]
    states = [[s[k] * coulomb_ref[k * HALF : (k + 1) * HALF] for k in range(2)] for s in states]
    states = [to_lanes(along_rows(s, tables)) for s in states]
    states = [along_lanes(s, tables) for s in states]
    return [[fold_rows(even + odd), fold_rows(even - odd)] for even, odd in states]


BACK_HI, BACK_LO, HART_HI, HART_LO, RIGHT, LEFT, PLACE, PLACE_T = 0, 1, 2, 3, 4, 6, 8, 9
TAG = 121
NEAR, FAR, SIB, VIA = 0, 3, 7, 11

T0, T1, T2, T3, S0, S1, S2, S3 = 0, FAR + 1, FAR + 2, FAR + 3, SIB, SIB + 1, SIB + 2, SIB + 3
STEPS = (
    ((1, T0, S0), (3, T0, S0)),
    ((1, T3, T1), (3, T3, T1)),
    ((1, S3, S1), (3, S3, S1)),
    ((2, T0, S0), (2, T3, T1)),
    ((2, S3, S1), (2, T2, S2)),
    ((1, T2, S2), (3, T2, S2)),
    ((0, T0, S0), (0, T3, T1)),
    ((0, S3, S1), (0, T2, S2)),
)


def pick(step, table):
    value = jnp.int32(table[0])
    for position, entry in enumerate(table):
        if position and entry != table[0]:
            value = jnp.where(step == position, jnp.int32(entry), value)
    return value


def kernel(
    coef_hbm, list_hbm, table_hbm, coulomb_hbm, out_ref,
    coef_ref, list_ref, tables, coulomb_ref, send_ref, got_ref, stick_ref, grids, fields, others,
    local_sem, send_sem, recv_sem,
):
    band = lax.axis_index("band")
    plane = lax.axis_index("plane")
    n_band = lax.axis_size("band")
    y, core = plane // 2, plane % 2
    z, x = band // 4, band % 4
    n_z = n_band // 4
    is_head, is_wrap = x == 0, x == 3

    def at_plane(dy, flip):
        return (band, (y + dy) % 4 * 2 + (core + flip) % 2)

    def at_band(t):
        return ((band + t + n_band) % n_band, plane)

    def at_chip(dz, dx):
        return ((z + dz + n_z) % n_z * 4 + (x + dx + 4) % 4, plane)

    next_target = (jnp.where(is_wrap, at_chip(0, 1)[0], at_band(1)[0]), plane)

    barrier = pltpu.get_barrier_semaphore()
    peers = [at_plane(dy, flip) for dy in range(4) for flip in range(2) if (dy, flip) != (0, 0)]
    peers += [at_band(t) for t in (1, 3, -1, -3)]
    peers += [at_chip(0, 1), at_chip(0, -1), at_chip(1, 0), at_chip(-1, 0), at_chip(1, 1), at_chip(-1, -1)]
    for peer in peers:
        pl.semaphore_signal(barrier, inc=1, device_id=peer, device_id_type=MESH)

    loads = [
        pltpu.make_async_copy(list_hbm, list_ref, local_sem.at[0]),
        pltpu.make_async_copy(coef_hbm, coef_ref, local_sem.at[1]),
        pltpu.make_async_copy(table_hbm.at[:4], tables.at[:4], local_sem.at[2]),
        pltpu.make_async_copy(table_hbm.at[4:], tables.at[4:], local_sem.at[3]),
        pltpu.make_async_copy(coulomb_hbm, coulomb_ref, local_sem.at[4]),
    ]
    for load in loads:
        load.start()
    for g in range(VIA + 1):
        for h in range(2):
            grids[g, h, ROWS:, :] = jnp.zeros((FULL - ROWS, HALF), F32)

    lane = lax.broadcasted_iota(jnp.int32, (CHUNK, HALF), 1)
    row = lax.broadcasted_iota(jnp.int32, (CHUNK, HALF), 0)
    loads[0].wait()
    listed = jnp.concatenate([list_ref[...].astype(F32), jnp.full((1, HALF - SLOTS), -1.0, F32)], 1)
    column = jnp.sum(jnp.where(lane == row, jnp.broadcast_to(listed, (CHUNK, HALF)), 0.0), axis=1, keepdims=True)
    tag = jnp.broadcast_to(column, (CHUNK, HALF))
    loads[1].wait()
    loads[2].wait()
    for b in range(BANDS):
        chunk = jnp.concatenate([coef_ref[:, b * N : (b + 1) * N], jnp.zeros((SLOTS, FULL - N), F32)], 1)
        chunk = jnp.concatenate([chunk, jnp.zeros((CHUNK - SLOTS, FULL), F32)], 0)
        hi, lo = split(chunk)
        moved = mm(jnp.concatenate([hi, lo], 0), tables[BACK_HI])
        moved = moved[:CHUNK] + moved[CHUNK:] + mm(hi, tables[BACK_LO])
        send_ref[b, 0] = jnp.where(lane == TAG, tag, moved[:, :HALF])
        send_ref[b, 1] = moved[:, HALF:]
    pl.semaphore_wait(barrier, len(peers))

    count = [0]
    copies = []

    def across(src, dst, send, recv, target):
        return pltpu.make_async_remote_copy(
            src_ref=src, dst_ref=dst, send_sem=send_sem.at[send], recv_sem=recv_sem.at[recv],
            device_id=target, device_id_type=MESH,
        )

    def plain(src, dst, target):
        copies.append(across(src, dst, count[0], count[0], target))
        count[0] += 1
        return copies[-1]

    chunk_copies = {}
    for h in range(2):
        for dy, flip in ((2, 0), (2, 1), (1, 0), (3, 0), (1, 1), (3, 1), (0, 1)):
            target = at_plane(dy, flip)
            slot = dy * 2 + flip
            args = (send_ref.at[target[1], h], got_ref.at[slot, h])
            chunk_copies[slot, h] = across(*args, count[0], count[0], target)
            count[0] += 1
            if h:
                chunk_copies[slot, 0].wait_send()
                copies.append(chunk_copies[slot, 1])
            chunk_copies[slot, h].start()
    got_ref[0] = send_ref[plane]

    def piece(ref, g, q):
        return ref.at[g, q // 2, pl.ds(q % 2 * HALF, ROWS - HALF if q % 2 else HALF)]

    def live(g, q):
        return piece(grids, g, q)

    def move(target, src, dst):
        return [plain(live(src, q), live(dst, q), target) for q in range(4)]

    near = {1: move(at_plane(1, 0), 0, NEAR + 1), 3: move(at_plane(3, 0), 0, NEAR + 3)}
    near[2] = [plain(live(NEAR + (3 if q % 2 else 1), q), live(NEAR + 2, q), at_plane(3 if q % 2 else 1, 0)) for q in range(4)]
    far = {3: move(at_band(3), 0, FAR + 3)}
    relay_at, via_at, far_at = count[0], count[0] + 4, count[0] + 8
    count[0] += 12
    relay = [across(live(VIA, q), live(FAR + 1, q), relay_at + q, far_at + q, at_chip(1, 0)) for q in range(2)]
    relayed = [across(live(VIA, q), live(VIA, q), via_at + q, via_at + q, at_chip(0, 1)) for q in range(2)]
    far[1] = [across(live(0, q), live(FAR + 1, q), far_at + q, far_at + q, at_band(1)) for q in range(4)]
    onward = [
        across(live(0, q), live(jnp.where(is_wrap, VIA, FAR + 1), q), far_at + q, jnp.where(is_wrap, via_at, far_at) + q, next_target)
        for q in range(2)
    ] + far[1][2:]
    skip_target = (jnp.where(is_head, at_chip(1, 1)[0], at_band(1)[0]), plane)
    from_lower = {
        0: plain(live(jnp.where(is_head, VIA, FAR + 1), 0), live(FAR + 2, 0), skip_target),
        2: across(live(FAR + 1, 2), live(FAR + 2, 2), count[0], count[0], at_band(1)),
    }
    from_upper = {2: across(live(FAR + 3, 2), live(FAR + 2, 2), count[0], count[0], at_band(-1))}
    count[0] += 1
    for q in (1, 3):
        from_upper[q] = plain(live(FAR + 3, q), live(FAR + 2, q), at_band(-1))
    far[2] = [(from_upper if q % 2 else from_lower)[q] for q in range(4)]
    sib = {
        t: [plain(grids.at[FAR + t if t else 0, h, :ROWS], grids.at[SIB + t, h, :ROWS], at_plane(0, 1)) for h in range(2)]
        for t in range(4)
    }

    stick_lane = lax.broadcasted_iota(jnp.int32, (HALF, FULL), 1).astype(F32)
    lane = lax.broadcasted_iota(jnp.int32, (FULL, HALF), 1)
    for h in range(2):
        phi = jnp.zeros((FULL, HALF), F32)
        for position, dy in enumerate((0, 1, 3, 2)):
            for flip in range(2):
                if (dy, flip) != (0, 0):
                    chunk_copies[dy * 2 + flip, h].wait_recv()
            rows = jnp.concatenate([got_ref[dy * 2, h], got_ref[dy * 2 + 1, h]], 0)
            if h == 0:
                picked = (jnp.broadcast_to(rows[:, TAG : TAG + 1], (HALF, FULL)) == stick_lane).astype(BF16)
                hart = jnp.concatenate([tables[HART_HI], tables[HART_LO]], 0)
                stick_ref[position] = mm_t(hart, picked).astype(BF16)
            hi, lo = split(rows)
            full = mm(stick_ref[position], jnp.concatenate([hi, lo], 1))
            full = full[:FULL] + full[FULL:]
            phi += full[:, :HALF] + full[:, HALF:]
        if h == 0:
            phi = jnp.where(lane < TAG, phi, 0.0)
        grids[0, h] = phi
        for first, second in ((2 * h, 2 * h + 1), (2 * h + 1, 2 * h)):
            onward[first].start()
            far[3][second].start()
        for first, second in ((2 * h, 2 * h + 1), (2 * h + 1, 2 * h)):
            near[1][first].start()
            near[3][second].start()
        sib[0][h].start()

    back = {
        1: [plain(piece(fields, 1, q), piece(others, 0, q), at_plane(3, 0)) for q in range(4)],
        3: [plain(piece(fields, 3, q), piece(others, 1, q), at_plane(1, 0)) for q in range(4)],
        2: [plain(piece(fields, 2, q), piece(others, 2, q), at_plane(3 if q < 2 else 1, 0)) for q in range(4)],
    }

    for n in range(4):
        fields[n] = jnp.zeros((2, FULL, HALF), F32)
    loads[3].wait()
    loads[4].wait()

    def received(parts):
        for part in parts:
            part.wait_recv()

    def started(parts):
        for part in parts:
            part.start()

    def pass_near(q):
        near[3 if q % 2 else 1][q].wait_recv()
        near[2][q].start()

    def from_below(q):
        @pl.when(is_head)
        def _():
            if q == 0:
                relayed[0].wait_recv()
                relay[0].start()
                from_lower[0].start()

        @pl.when(jnp.logical_not(is_head))
        def _():
            far[1][q].wait_recv()
            from_lower[q].start()

    def from_above(q):
        far[3][q].wait_recv()
        from_upper[q].start()

        @pl.when(is_head)
        def _():
            if q == 1:
                relayed[1].wait_recv()
                relay[1].start()

        @pl.when(x == 2)
        def _():
            if q == 3:
                far[3][2].wait_recv()
                from_upper[2].start()

    def share(h):
        if h == 0:
            far[3][0].wait_recv()
        else:
            pl.when(x != 2)(far[3][2].wait_recv)
        sib[3][h].start()

        @pl.when(jnp.logical_not(is_head))
        def _():
            far[1][2 * h + 1].wait_recv()
            sib[1][h].start()

    def share_far(h):
        received(far[2][2 * h : 2 * h + 2])
        sib[2][h].start()

    def before_0():
        from_below(0)
        from_above(1)
        share(0)
        pass_near(0)
        pass_near(1)
        from_below(2)
        from_above(3)
        share(1)
        pass_near(2)
        pass_near(3)
        received((near[1][1], near[1][3], near[3][0], near[3][2]))
        received(sib[0])

    def before_1():
        @pl.when(is_head)
        def _():
            received(far[1])
            started(sib[1])

    def before_2():
        share_far(0)
        received(sib[3])
        received(sib[1])

    def before_3():
        share_far(1)
        received(near[2])

    def before_4():
        received(sib[2])

    def after_4():
        started(back[2])

    def after_5():
        started(back[1][2:])
        started(back[3][:2])

    def merge(n, q):
        back[2][q].wait_recv()
        piece(fields, n, q)[...] += piece(others, 2, q)[...]
        back[n][q].start()

    def after_7():
        for q in range(2):
            merge(1, q)
            merge(3, 2 + q)

    before = {0: before_0, 1: before_1, 2: before_2, 3: before_3, 4: before_4}
    after = {4: after_4, 5: after_5, 7: after_7}

    def body(step, carry):
        for k, action in before.items():
            pl.when(step == k)(action)
        pairs, places = [], []
        for part in range(2):
            n = pick(step, [s[part][0] for s in STEPS])
            own = [grids[n, h] for h in range(2)]
            for k in (1, 2):
                g = pick(step, [s[part][k] for s in STEPS])
                pairs.append((own, [grids[g, h] for h in range(2)]))
            places.append(n)
        values = potentials(pairs, tables, coulomb_ref)
        for part, n in enumerate(places):
            for h in range(2):
                first, second = 2 * part, 2 * part + 1
                fields[n, h] += values[first][h] * pairs[first][1][h] + values[second][h] * pairs[second][1][h]
        for k, action in after.items():
            pl.when(step == k)(action)
        return carry

    lax.fori_loop(0, len(STEPS), body, 0)

    received(back[1])
    received(back[3])
    halves = []
    for h in range(2):
        half = fields[0, h, :ROWS] + others[0, h, :ROWS] + others[1, h, :ROWS]
        halves.append(jnp.concatenate([half, jnp.zeros((FULL - ROWS, HALF), F32)], 0))
    hi, lo = split(jnp.concatenate(halves, 1))
    ordered = mm_t(tables[PLACE_T], hi) + mm_t(tables[PLACE_T], lo)
    hi, lo = split(ordered)
    ordered = mm(hi, tables[PLACE]) + mm(lo, tables[PLACE])
    out_ref[0] = ordered[:N, :N]

    def sent(parts):
        for part in parts:
            part.wait_send()

    sent(onward)
    pl.when(is_head)(functools.partial(sent, relay))
    pl.when(jnp.logical_not(is_head))(from_lower[2].wait_send)
    pl.when(x == 2)(from_upper[2].wait_send)
    for copy in copies:
        copy.wait_send()


def on_device(stick_coef, stick_list):
    tables, coulomb = make_tables()
    tables = jnp.asarray(tables.reshape(10, FULL, FULL))
    dma = pltpu.SemaphoreType.DMA
    return pl.pallas_call(
        kernel,
        out_shape=jax.ShapeDtypeStruct((1, N, N), F32),
        in_specs=[pl.BlockSpec(memory_space=pltpu.HBM)] * 4,
        out_specs=pl.BlockSpec(memory_space=pltpu.VMEM),
        scratch_shapes=[
            pltpu.VMEM((SLOTS, BANDS * N), F32),
            pltpu.VMEM((1, SLOTS), jnp.int32),
            pltpu.VMEM((10, FULL, FULL), BF16),
            pltpu.VMEM((FULL, FULL), F32),
            pltpu.VMEM((BANDS, 2, CHUNK, HALF), F32),
            pltpu.VMEM((BANDS, 2, CHUNK, HALF), F32),
            pltpu.VMEM((4, 2 * FULL, HALF), BF16),
            pltpu.VMEM((VIA + 1, 2, FULL, HALF), F32),
            pltpu.VMEM((4, 2, FULL, HALF), F32),
            pltpu.VMEM((3, 2, FULL, HALF), F32),
            dma((5,)),
            dma((84,)),
            dma((84,)),
        ],
        compiler_params=pltpu.CompilerParams(
            collective_id=0, has_side_effects=True, vmem_limit_bytes=60 * 1024 * 1024
        ),
    )(stick_coef, stick_list.reshape(1, SLOTS), tables, jnp.asarray(coulomb))


def solution(mesh):
    in_specs = (P("plane", "band"), P("plane"))
    out_specs = P(("band", "plane"), None, None)
    return jax.shard_map(on_device, mesh=mesh, in_specs=in_specs, out_specs=out_specs, check_vma=False)
```

```python
import functools
import math

import jax
import jax.numpy as jnp
import ml_dtypes
import numpy as np
from jax import lax
from jax.experimental import pallas as pl
from jax.experimental.pallas import tpu as pltpu
from jax.sharding import PartitionSpec as P

N = 240
HALF = 128
FULL = 256
ROWS = 248
SLOTS = 60
CHUNK = 64
BANDS = 8
MESH = pl.DeviceIdType.MESH
F32 = jnp.float32
BF16 = jnp.bfloat16


def split_np(values):
    high = values.astype(np.float32).astype(ml_dtypes.bfloat16)
    low = (values - high.astype(np.float64)).astype(np.float32).astype(ml_dtypes.bfloat16)
    return high, low


def make_tables():
    spot = -np.ones(FULL, np.int64)
    spot[:121] = np.arange(121)
    spot[HALF + 1 : HALF + 120] = N - np.arange(1, 120)
    index = np.arange(N)
    phase = (index[:, None] * index[None, :] % N) * (2.0 * np.pi / N)
    hart = (np.cos(phase) + np.sin(phase)) / math.sqrt(N)
    folded = np.zeros((FULL, FULL))
    folded[spot >= 0, :N] = hart[spot[spot >= 0]]
    f_hi, f_lo = split_np(folded)
    cosine = np.zeros((HALF, HALF))
    cosine[:121, :121] = np.cos(phase[:121, :121]) / math.sqrt(N)
    sine = np.zeros((HALF, HALF))
    sine[1:120, 1:120] = np.sin(phase[1:120, 1:120]) / math.sqrt(N)
    right, left = [], []
    for table in (cosine, sine):
        hi, lo = split_np(table)
        right.append(np.block([[hi, lo], [hi, lo]]))
        left.append(np.block([[hi, hi], [lo, lo]]))
    freq = np.arange(HALF).astype(np.float64)
    weight = np.where((freq == 0) | (freq == 120), 1.0, 2.0)
    squared = freq[:, None] ** 2 + freq[None, :] ** 2
    coulomb = np.where(squared > 0, 0.25 * N / np.maximum(squared, 1.0), 0.0)
    coulomb = coulomb * weight[:, None] * weight[None, :]
    even = (freq <= 120).astype(np.float64)
    odd = ((freq >= 1) & (freq <= 119)).astype(np.float64)
    live = np.concatenate([even, odd])
    coulomb = (np.tile(coulomb, (2, 2)) * live[:, None] * live[None, :]).astype(np.float32)
    place = np.zeros((FULL, FULL), np.float32)
    for p in range(FULL):
        if spot[p] >= 0:
            place[p, spot[p]] = 1.0
    bf16 = ml_dtypes.bfloat16
    blocks = [f_hi.T, f_lo.T, f_hi, f_lo, *right, *left, place.astype(bf16), place.T.astype(bf16)]
    return np.concatenate(blocks, 0), coulomb


def split(values):
    high = values.astype(BF16)
    low = (values - high.astype(F32)).astype(BF16)
    return high, low


def mm(lhs, rhs):
    return lax.dot_general(lhs, rhs, (((1,), (0,)), ((), ())), preferred_element_type=F32)


def mm_t(lhs, rhs):
    return lax.dot_general(lhs, rhs, (((1,), (1,)), ((), ())), preferred_element_type=F32)


def along_lanes(halves, tables):
    out = []
    for p in range(2):
        hi, lo = split(halves[p])
        full = mm(jnp.concatenate([hi, lo], 1), tables[RIGHT + p])
        out.append(full[:, :HALF] + full[:, HALF:])
    return out


def along_rows(halves, tables):
    out = []
    for p in range(2):
        hi, lo = split(halves[p])
        full = mm(tables[LEFT + p], jnp.concatenate([hi, lo], 0))
        out.append(full[:HALF] + full[HALF:])
    return out


def to_rows(pair):
    return [jnp.concatenate([pair[0][k * HALF : (k + 1) * HALF], pair[1][k * HALF : (k + 1) * HALF]], 1) for k in range(2)]


def to_lanes(pair):
    return [jnp.concatenate([pair[0][:, k * HALF : (k + 1) * HALF], pair[1][:, k * HALF : (k + 1) * HALF]], 0) for k in range(2)]


def fold_rows(values):
    return jnp.concatenate([values[:HALF] + values[HALF:], values[:HALF] - values[HALF:]], 0)


def potentials(pairs, tables, coulomb_ref):
    states = []
    for own, partner in pairs:
        plus, minus = own[0] * partner[0], own[1] * partner[1]
        states.append([fold_rows(plus + minus), fold_rows(plus - minus)])
    states = [to_rows(along_lanes(s, tables)) for s in states]
    states = [along_rows(s, tables) for s in states]
    states = [[s[k] * coulomb_ref[k * HALF : (k + 1) * HALF] for k in range(2)] for s in states]
    states = [to_lanes(along_rows(s, tables)) for s in states]
    states = [along_lanes(s, tables) for s in states]
    return [[fold_rows(even + odd), fold_rows(even - odd)] for even, odd in states]


BACK_HI, BACK_LO, HART_HI, HART_LO, RIGHT, LEFT, PLACE, PLACE_T = 0, 1, 2, 3, 4, 6, 8, 9
TAG = 121
NEAR, FAR, SIB, VIA = 0, 3, 7, 11

T0, T1, T2, T3, S0, S1, S2, S3 = 0, FAR + 1, FAR + 2, FAR + 3, SIB, SIB + 1, SIB + 2, SIB + 3
STEPS = (
    ((1, T0, S0), (3, T0, S0)),
    ((1, T3, T1), (3, T3, T1)),
    ((1, S3, S1), (3, S3, S1)),
    ((2, T0, S0), (2, T3, T1)),
    ((2, S3, S1), (2, T2, S2)),
    ((1, T2, S2), (3, T2, S2)),
    ((0, T0, S0), (0, T3, T1)),
    ((0, S3, S1), (0, T2, S2)),
)


def pick(step, table):
    value = jnp.int32(table[0])
    for position, entry in enumerate(table):
        if position and entry != table[0]:
            value = jnp.where(step == position, jnp.int32(entry), value)
    return value


def kernel(
    coef_hbm, list_hbm, table_hbm, coulomb_hbm, out_ref,
    coef_ref, list_ref, tables, coulomb_ref, send_ref, got_ref, stick_ref, grids, fields, others,
    local_sem, send_sem, recv_sem,
):
    band = lax.axis_index("band")
    plane = lax.axis_index("plane")
    n_band = lax.axis_size("band")
    y, core = plane // 2, plane % 2
    z, x = band // 4, band % 4
    n_z = n_band // 4
    is_head, is_wrap = x == 0, x == 3

    def at_plane(dy, flip):
        return (band, (y + dy) % 4 * 2 + (core + flip) % 2)

    def at_band(t):
        return ((band + t + n_band) % n_band, plane)

    def at_chip(dz, dx):
        return ((z + dz + n_z) % n_z * 4 + (x + dx + 4) % 4, plane)

    next_target = (jnp.where(is_wrap, at_chip(0, 1)[0], at_band(1)[0]), plane)

    barrier = pltpu.get_barrier_semaphore()
    peers = [at_plane(dy, flip) for dy in range(4) for flip in range(2) if (dy, flip) != (0, 0)]
    peers += [at_band(t) for t in (1, 3, -1, -3)]
    peers += [at_chip(0, 1), at_chip(0, -1), at_chip(1, 0), at_chip(-1, 0), at_chip(1, 1), at_chip(-1, -1)]
    for peer in peers:
        pl.semaphore_signal(barrier, inc=1, device_id=peer, device_id_type=MESH)

    loads = [
        pltpu.make_async_copy(list_hbm, list_ref, local_sem.at[0]),
        pltpu.make_async_copy(coef_hbm, coef_ref, local_sem.at[1]),
        pltpu.make_async_copy(table_hbm.at[:2], tables.at[:2], local_sem.at[2]),
        pltpu.make_async_copy(table_hbm.at[2:], tables.at[2:], local_sem.at[3]),
        pltpu.make_async_copy(coulomb_hbm, coulomb_ref, local_sem.at[4]),
    ]
    for load in loads[:3]:
        load.start()
    for g in range(VIA + 1):
        for h in range(2):
            grids[g, h, ROWS:, :] = jnp.zeros((FULL - ROWS, HALF), F32)

    lane = lax.broadcasted_iota(jnp.int32, (CHUNK, HALF), 1)
    row = lax.broadcasted_iota(jnp.int32, (CHUNK, HALF), 0)
    loads[0].wait()
    listed = jnp.concatenate([list_ref[...].astype(F32), jnp.full((1, HALF - SLOTS), -1.0, F32)], 1)
    column = jnp.sum(jnp.where(lane == row, jnp.broadcast_to(listed, (CHUNK, HALF)), 0.0), axis=1, keepdims=True)
    tag = jnp.broadcast_to(column, (CHUNK, HALF))
    loads[1].wait()
    loads[2].wait()
    for load in loads[3:]:
        load.start()
    for b in range(BANDS):
        chunk = jnp.concatenate([coef_ref[:, b * N : (b + 1) * N], jnp.zeros((SLOTS, FULL - N), F32)], 1)
        chunk = jnp.concatenate([chunk, jnp.zeros((CHUNK - SLOTS, FULL), F32)], 0)
        hi, lo = split(chunk)
        moved = mm(jnp.concatenate([hi, lo], 0), tables[BACK_HI])
        moved = moved[:CHUNK] + moved[CHUNK:] + mm(hi, tables[BACK_LO])
        send_ref[b, 0] = jnp.where(lane == TAG, tag, moved[:, :HALF])
        send_ref[b, 1] = moved[:, HALF:]
    pl.semaphore_wait(barrier, len(peers))

    count = [0]
    copies = []

    def across(src, dst, send, recv, target):
        return pltpu.make_async_remote_copy(
            src_ref=src, dst_ref=dst, send_sem=send_sem.at[send], recv_sem=recv_sem.at[recv],
            device_id=target, device_id_type=MESH,
        )

    def plain(src, dst, target):
        copies.append(across(src, dst, count[0], count[0], target))
        count[0] += 1
        return copies[-1]

    chunk_copies = {}
    for h in range(2):
        for dy, flip in ((2, 0), (2, 1), (1, 0), (3, 0), (1, 1), (3, 1), (0, 1)):
            target = at_plane(dy, flip)
            slot = dy * 2 + flip
            args = (send_ref.at[target[1], h], got_ref.at[slot, h])
            chunk_copies[slot, h] = across(*args, count[0], count[0], target)
            count[0] += 1
            if h:
                chunk_copies[slot, 0].wait_send()
                copies.append(chunk_copies[slot, 1])
            chunk_copies[slot, h].start()
    got_ref[0] = send_ref[plane]
    for n in range(4):
        fields[n] = jnp.zeros((2, FULL, HALF), F32)

    def piece(ref, g, q):
        return ref.at[g, q // 2, pl.ds(q % 2 * HALF, ROWS - HALF if q % 2 else HALF)]

    def live(g, q):
        return piece(grids, g, q)

    def move(target, src, dst):
        return [plain(live(src, q), live(dst, q), target) for q in range(4)]

    near = {1: move(at_plane(1, 0), 0, NEAR + 1), 3: move(at_plane(3, 0), 0, NEAR + 3)}
    near[2] = [plain(live(NEAR + (3 if q % 2 else 1), q), live(NEAR + 2, q), at_plane(3 if q % 2 else 1, 0)) for q in range(4)]
    far = {3: move(at_band(3), 0, FAR + 3)}
    relay_at, via_at, far_at = count[0], count[0] + 4, count[0] + 8
    count[0] += 12
    relay = [across(live(VIA, q), live(FAR + 1, q), relay_at + q, far_at + q, at_chip(1, 0)) for q in range(2)]
    relayed = [across(live(VIA, q), live(VIA, q), via_at + q, via_at + q, at_chip(0, 1)) for q in range(2)]
    far[1] = [across(live(0, q), live(FAR + 1, q), far_at + q, far_at + q, at_band(1)) for q in range(4)]
    onward = [
        across(live(0, q), live(jnp.where(is_wrap, VIA, FAR + 1), q), far_at + q, jnp.where(is_wrap, via_at, far_at) + q, next_target)
        for q in range(2)
    ] + far[1][2:]
    skip_target = (jnp.where(is_head, at_chip(1, 1)[0], at_band(1)[0]), plane)
    from_lower = {
        0: plain(live(jnp.where(is_head, VIA, FAR + 1), 0), live(FAR + 2, 0), skip_target),
        2: across(live(FAR + 1, 2), live(FAR + 2, 2), count[0], count[0], at_band(1)),
    }
    from_upper = {2: across(live(FAR + 3, 2), live(FAR + 2, 2), count[0], count[0], at_band(-1))}
    count[0] += 1
    for q in (1, 3):
        from_upper[q] = plain(live(FAR + 3, q), live(FAR + 2, q), at_band(-1))
    far[2] = [(from_upper if q % 2 else from_lower)[q] for q in range(4)]
    sib = {
        t: [plain(grids.at[FAR + t if t else 0, h, :ROWS], grids.at[SIB + t, h, :ROWS], at_plane(0, 1)) for h in range(2)]
        for t in range(4)
    }

    loads[3].wait()
    loads[4].wait()
    stick_lane = lax.broadcasted_iota(jnp.int32, (HALF, FULL), 1).astype(F32)
    lane = lax.broadcasted_iota(jnp.int32, (FULL, HALF), 1)
    for h in range(2):
        phi = jnp.zeros((FULL, HALF), F32)
        for position, dy in enumerate((0, 1, 3, 2)):
            for flip in range(2):
                if (dy, flip) != (0, 0):
                    chunk_copies[dy * 2 + flip, h].wait_recv()
            rows = jnp.concatenate([got_ref[dy * 2, h], got_ref[dy * 2 + 1, h]], 0)
            if h == 0:
                picked = (jnp.broadcast_to(rows[:, TAG : TAG + 1], (HALF, FULL)) == stick_lane).astype(BF16)
                hart = jnp.concatenate([tables[HART_HI], tables[HART_LO]], 0)
                stick_ref[position] = mm_t(hart, picked).astype(BF16)
            hi, lo = split(rows)
            full = mm(stick_ref[position], jnp.concatenate([hi, lo], 1))
            full = full[:FULL] + full[FULL:]
            phi += full[:, :HALF] + full[:, HALF:]
        if h == 0:
            phi = jnp.where(lane < TAG, phi, 0.0)
        grids[0, h] = phi
        for first, second in ((2 * h, 2 * h + 1), (2 * h + 1, 2 * h)):
            onward[first].start()
            far[3][second].start()
        for first, second in ((2 * h, 2 * h + 1), (2 * h + 1, 2 * h)):
            near[1][first].start()
            near[3][second].start()
        sib[0][h].start()

    back = {
        1: [plain(piece(fields, 1, q), piece(others, 0, q), at_plane(3, 0)) for q in range(4)],
        3: [plain(piece(fields, 3, q), piece(others, 1, q), at_plane(1, 0)) for q in range(4)],
        2: [plain(piece(fields, 2, q), piece(others, 2, q), at_plane(3 if q < 2 else 1, 0)) for q in range(4)],
    }


    def received(parts):
        for part in parts:
            part.wait_recv()

    def started(parts):
        for part in parts:
            part.start()

    def pass_near(q):
        near[3 if q % 2 else 1][q].wait_recv()
        near[2][q].start()

    def from_below(q):
        @pl.when(is_head)
        def _():
            if q == 0:
                relayed[0].wait_recv()
                relay[0].start()
                from_lower[0].start()

        @pl.when(jnp.logical_not(is_head))
        def _():
            far[1][q].wait_recv()
            from_lower[q].start()

    def from_above(q):
        far[3][q].wait_recv()
        from_upper[q].start()

        @pl.when(is_head)
        def _():
            if q == 1:
                relayed[1].wait_recv()
                relay[1].start()

        @pl.when(x == 2)
        def _():
            if q == 3:
                far[3][2].wait_recv()
                from_upper[2].start()

    def share(h):
        if h == 0:
            far[3][0].wait_recv()
        else:
            pl.when(x != 2)(far[3][2].wait_recv)
        sib[3][h].start()

        @pl.when(jnp.logical_not(is_head))
        def _():
            far[1][2 * h + 1].wait_recv()
            sib[1][h].start()

    def share_far(h):
        received(far[2][2 * h : 2 * h + 2])
        sib[2][h].start()

    def before_0():
        from_below(0)
        from_above(1)
        share(0)
        pass_near(0)
        pass_near(1)
        from_below(2)
        from_above(3)
        share(1)
        pass_near(2)
        pass_near(3)
        received((near[1][1], near[1][3], near[3][0], near[3][2]))
        received(sib[0])

    def before_1():
        @pl.when(is_head)
        def _():
            received(far[1])
            started(sib[1])

    def before_2():
        share_far(0)
        received(sib[3])
        received(sib[1])

    def before_3():
        share_far(1)
        received(near[2])

    def before_4():
        received(sib[2])

    def after_4():
        started(back[2])

    def after_5():
        started(back[1][2:])
        started(back[3][:2])

    def merge(n, q):
        back[2][q].wait_recv()
        piece(fields, n, q)[...] += piece(others, 2, q)[...]
        back[n][q].start()

    def after_7():
        for q in range(2):
            merge(1, q)
            merge(3, 2 + q)

    before = {0: before_0, 1: before_1, 2: before_2, 3: before_3, 4: before_4}
    after = {4: after_4, 5: after_5, 7: after_7}

    def body(step, carry):
        for k, action in before.items():
            pl.when(step == k)(action)
        pairs, places = [], []
        for part in range(2):
            n = pick(step, [s[part][0] for s in STEPS])
            own = [grids[n, h] for h in range(2)]
            for k in (1, 2):
                g = pick(step, [s[part][k] for s in STEPS])
                pairs.append((own, [grids[g, h] for h in range(2)]))
            places.append(n)
        values = potentials(pairs, tables, coulomb_ref)
        for part, n in enumerate(places):
            for h in range(2):
                first, second = 2 * part, 2 * part + 1
                fields[n, h] += values[first][h] * pairs[first][1][h] + values[second][h] * pairs[second][1][h]
        for k, action in after.items():
            pl.when(step == k)(action)
        return carry

    lax.fori_loop(0, len(STEPS), body, 0)

    received(back[1])
    received(back[3])
    halves = []
    for h in range(2):
        half = fields[0, h, :ROWS] + others[0, h, :ROWS] + others[1, h, :ROWS]
        halves.append(jnp.concatenate([half, jnp.zeros((FULL - ROWS, HALF), F32)], 0))
    hi, lo = split(jnp.concatenate(halves, 1))
    ordered = mm_t(tables[PLACE_T], hi) + mm_t(tables[PLACE_T], lo)
    hi, lo = split(ordered)
    ordered = mm(hi, tables[PLACE]) + mm(lo, tables[PLACE])
    out_ref[0] = ordered[:N, :N]

    def sent(parts):
        for part in parts:
            part.wait_send()

    sent(onward)
    pl.when(is_head)(functools.partial(sent, relay))
    pl.when(jnp.logical_not(is_head))(from_lower[2].wait_send)
    pl.when(x == 2)(from_upper[2].wait_send)
    for copy in copies:
        copy.wait_send()


def on_device(stick_coef, stick_list):
    tables, coulomb = make_tables()
    tables = jnp.asarray(tables.reshape(10, FULL, FULL))
    dma = pltpu.SemaphoreType.DMA
    return pl.pallas_call(
        kernel,
        out_shape=jax.ShapeDtypeStruct((1, N, N), F32),
        in_specs=[pl.BlockSpec(memory_space=pltpu.HBM)] * 4,
        out_specs=pl.BlockSpec(memory_space=pltpu.VMEM),
        scratch_shapes=[
            pltpu.VMEM((SLOTS, BANDS * N), F32),
            pltpu.VMEM((1, SLOTS), jnp.int32),
            pltpu.VMEM((10, FULL, FULL), BF16),
            pltpu.VMEM((FULL, FULL), F32),
            pltpu.VMEM((BANDS, 2, CHUNK, HALF), F32),
            pltpu.VMEM((BANDS, 2, CHUNK, HALF), F32),
            pltpu.VMEM((4, 2 * FULL, HALF), BF16),
            pltpu.VMEM((VIA + 1, 2, FULL, HALF), F32),
            pltpu.VMEM((4, 2, FULL, HALF), F32),
            pltpu.VMEM((3, 2, FULL, HALF), F32),
            dma((5,)),
            dma((84,)),
            dma((84,)),
        ],
        compiler_params=pltpu.CompilerParams(
            collective_id=0, has_side_effects=True, vmem_limit_bytes=60 * 1024 * 1024
        ),
    )(stick_coef, stick_list.reshape(1, SLOTS), tables, jnp.asarray(coulomb))


def solution(mesh):
    in_specs = (P("plane", "band"), P("plane"))
    out_specs = P(("band", "plane"), None, None)
    return jax.shard_map(on_device, mesh=mesh, in_specs=in_specs, out_specs=out_specs, check_vma=False)
```

```python
import functools
import math

import jax
import jax.numpy as jnp
import ml_dtypes
import numpy as np
from jax import lax
from jax.experimental import pallas as pl
from jax.experimental.pallas import tpu as pltpu
from jax.sharding import PartitionSpec as P

N = 240
HALF = 128
FULL = 256
ROWS = 248
SLOTS = 60
CHUNK = 64
BANDS = 8
MESH = pl.DeviceIdType.MESH
F32 = jnp.float32
BF16 = jnp.bfloat16


def split_np(values):
    high = values.astype(np.float32).astype(ml_dtypes.bfloat16)
    low = (values - high.astype(np.float64)).astype(np.float32).astype(ml_dtypes.bfloat16)
    return high, low


def make_tables():
    spot = -np.ones(FULL, np.int64)
    spot[:121] = np.arange(121)
    spot[HALF + 1 : HALF + 120] = N - np.arange(1, 120)
    index = np.arange(N)
    phase = (index[:, None] * index[None, :] % N) * (2.0 * np.pi / N)
    hart = (np.cos(phase) + np.sin(phase)) / math.sqrt(N)
    folded = np.zeros((FULL, FULL))
    folded[spot >= 0, :N] = hart[spot[spot >= 0]]
    f_hi, f_lo = split_np(folded)
    cosine = np.zeros((HALF, HALF))
    cosine[:121, :121] = np.cos(phase[:121, :121]) / math.sqrt(N)
    sine = np.zeros((HALF, HALF))
    sine[1:120, 1:120] = np.sin(phase[1:120, 1:120]) / math.sqrt(N)
    right, left = [], []
    for table in (cosine, sine):
        hi, lo = split_np(table)
        right.append(np.block([[hi, lo], [hi, lo]]))
        left.append(np.block([[hi, hi], [lo, lo]]))
    freq = np.arange(HALF).astype(np.float64)
    weight = np.where((freq == 0) | (freq == 120), 1.0, 2.0)
    squared = freq[:, None] ** 2 + freq[None, :] ** 2
    coulomb = np.where(squared > 0, 0.25 * N / np.maximum(squared, 1.0), 0.0)
    coulomb = coulomb * weight[:, None] * weight[None, :]
    even = (freq <= 120).astype(np.float64)
    odd = ((freq >= 1) & (freq <= 119)).astype(np.float64)
    live = np.concatenate([even, odd])
    coulomb = (np.tile(coulomb, (2, 2)) * live[:, None] * live[None, :]).astype(np.float32)
    place = np.zeros((FULL, FULL), np.float32)
    for p in range(FULL):
        if spot[p] >= 0:
            place[p, spot[p]] = 1.0
    bf16 = ml_dtypes.bfloat16
    blocks = [f_hi.T, f_lo.T, f_hi, f_lo, *right, *left, place.astype(bf16), place.T.astype(bf16)]
    return np.concatenate(blocks, 0), coulomb


def split(values):
    high = values.astype(BF16)
    low = (values - high.astype(F32)).astype(BF16)
    return high, low


def mm(lhs, rhs):
    return lax.dot_general(lhs, rhs, (((1,), (0,)), ((), ())), preferred_element_type=F32)


def mm_t(lhs, rhs):
    return lax.dot_general(lhs, rhs, (((1,), (1,)), ((), ())), preferred_element_type=F32)


def along_lanes(halves, tables):
    out = []
    for p in range(2):
        hi, lo = split(halves[p])
        full = mm(jnp.concatenate([hi, lo], 1), tables[RIGHT + p])
        out.append(full[:, :HALF] + full[:, HALF:])
    return out


def along_rows(halves, tables):
    out = []
    for p in range(2):
        hi, lo = split(halves[p])
        full = mm(tables[LEFT + p], jnp.concatenate([hi, lo], 0))
        out.append(full[:HALF] + full[HALF:])
    return out


def to_rows(pair):
    return [jnp.concatenate([pair[0][k * HALF : (k + 1) * HALF], pair[1][k * HALF : (k + 1) * HALF]], 1) for k in range(2)]


def to_lanes(pair):
    return [jnp.concatenate([pair[0][:, k * HALF : (k + 1) * HALF], pair[1][:, k * HALF : (k + 1) * HALF]], 0) for k in range(2)]


def fold_rows(values):
    return jnp.concatenate([values[:HALF] + values[HALF:], values[:HALF] - values[HALF:]], 0)


def potentials(pairs, tables, coulomb_ref):
    states = []
    for own, partner in pairs:
        plus, minus = own[0] * partner[0], own[1] * partner[1]
        states.append([fold_rows(plus + minus), fold_rows(plus - minus)])
    states = [to_rows(along_lanes(s, tables)) for s in states]
    states = [along_rows(s, tables) for s in states]
    states = [[s[k] * coulomb_ref[k * HALF : (k + 1) * HALF] for k in range(2)] for s in states]
    states = [to_lanes(along_rows(s, tables)) for s in states]
    states = [along_lanes(s, tables) for s in states]
    return [[fold_rows(even + odd), fold_rows(even - odd)] for even, odd in states]


BACK_HI, BACK_LO, HART_HI, HART_LO, RIGHT, LEFT, PLACE, PLACE_T = 0, 1, 2, 3, 4, 6, 8, 9
TAG = 121
NEAR, FAR, SIB, VIA = 0, 3, 7, 11

STEPS = (
    ((1, 0), (3, 0)),
    ((1, 3), (3, 3)),
    ((2, 0), (2, 3)),
    ((1, 1), (3, 1)),
    ((2, 1), (2, 2)),
    ((1, 2), (3, 2)),
    ((0, 0), (0, 3)),
    ((0, 1), (0, 2)),
)


def pick(step, table):
    value = jnp.int32(table[0])
    for position, entry in enumerate(table):
        if position and entry != table[0]:
            value = jnp.where(step == position, jnp.int32(entry), value)
    return value


def kernel(
    coef_hbm, list_hbm, table_hbm, coulomb_hbm, out_ref,
    coef_ref, list_ref, tables, coulomb_ref, send_ref, got_ref, stick_ref, grids, fields, others,
    local_sem, send_sem, recv_sem,
):
    band = lax.axis_index("band")
    plane = lax.axis_index("plane")
    n_band = lax.axis_size("band")
    y, core = plane // 2, plane % 2
    z, x = band // 4, band % 4
    n_z = n_band // 4
    is_head, is_wrap = x == 0, x == 3

    def at_plane(dy, flip):
        return (band, (y + dy) % 4 * 2 + (core + flip) % 2)

    def at_band(t):
        return ((band + t + n_band) % n_band, plane)

    def at_chip(dz, dx):
        return ((z + dz + n_z) % n_z * 4 + (x + dx + 4) % 4, plane)

    next_target = (jnp.where(is_wrap, at_chip(0, 1)[0], at_band(1)[0]), plane)

    barrier = pltpu.get_barrier_semaphore()
    peers = [at_plane(dy, flip) for dy in range(4) for flip in range(2) if (dy, flip) != (0, 0)]
    peers += [at_band(t) for t in (1, 3, -1, -3)]
    peers += [at_chip(0, 1), at_chip(0, -1), at_chip(1, 0), at_chip(-1, 0), at_chip(1, 1), at_chip(-1, -1)]
    for peer in peers:
        pl.semaphore_signal(barrier, inc=1, device_id=peer, device_id_type=MESH)

    loads = [
        pltpu.make_async_copy(list_hbm, list_ref, local_sem.at[0]),
        pltpu.make_async_copy(coef_hbm, coef_ref, local_sem.at[1]),
        pltpu.make_async_copy(table_hbm.at[:4], tables.at[:4], local_sem.at[2]),
        pltpu.make_async_copy(table_hbm.at[4:], tables.at[4:], local_sem.at[3]),
        pltpu.make_async_copy(coulomb_hbm, coulomb_ref, local_sem.at[4]),
    ]
    for load in loads:
        load.start()
    for g in range(VIA + 1):
        for h in range(2):
            grids[g, h, ROWS:, :] = jnp.zeros((FULL - ROWS, HALF), F32)

    lane = lax.broadcasted_iota(jnp.int32, (CHUNK, HALF), 1)
    row = lax.broadcasted_iota(jnp.int32, (CHUNK, HALF), 0)
    loads[0].wait()
    listed = jnp.concatenate([list_ref[...].astype(F32), jnp.full((1, HALF - SLOTS), -1.0, F32)], 1)
    column = jnp.sum(jnp.where(lane == row, jnp.broadcast_to(listed, (CHUNK, HALF)), 0.0), axis=1, keepdims=True)
    tag = jnp.broadcast_to(column, (CHUNK, HALF))
    loads[1].wait()
    loads[2].wait()
    for b in range(BANDS):
        chunk = jnp.concatenate([coef_ref[:, b * N : (b + 1) * N], jnp.zeros((SLOTS, FULL - N), F32)], 1)
        chunk = jnp.concatenate([chunk, jnp.zeros((CHUNK - SLOTS, FULL), F32)], 0)
        hi, lo = split(chunk)
        moved = mm(jnp.concatenate([hi, lo], 0), tables[BACK_HI])
        moved = moved[:CHUNK] + moved[CHUNK:] + mm(hi, tables[BACK_LO])
        send_ref[b, 0] = jnp.where(lane == TAG, tag, moved[:, :HALF])
        send_ref[b, 1] = moved[:, HALF:]
    pl.semaphore_wait(barrier, len(peers))

    count = [0]
    copies = []

    def across(src, dst, send, recv, target):
        return pltpu.make_async_remote_copy(
            src_ref=src, dst_ref=dst, send_sem=send_sem.at[send], recv_sem=recv_sem.at[recv],
            device_id=target, device_id_type=MESH,
        )

    def plain(src, dst, target):
        copies.append(across(src, dst, count[0], count[0], target))
        count[0] += 1
        return copies[-1]

    chunk_copies = {}
    for h in range(2):
        for dy, flip in ((2, 0), (2, 1), (1, 0), (3, 0), (1, 1), (3, 1), (0, 1)):
            target = at_plane(dy, flip)
            slot = dy * 2 + flip
            args = (send_ref.at[target[1], h], got_ref.at[slot, h])
            chunk_copies[slot, h] = across(*args, count[0], count[0], target)
            count[0] += 1
            if h:
                chunk_copies[slot, 0].wait_send()
                copies.append(chunk_copies[slot, 1])
            chunk_copies[slot, h].start()
    got_ref[0] = send_ref[plane]

    def piece(ref, g, q):
        return ref.at[g, q // 2, pl.ds(q % 2 * HALF, ROWS - HALF if q % 2 else HALF)]

    def live(g, q):
        return piece(grids, g, q)

    def move(target, src, dst):
        return [plain(live(src, q), live(dst, q), target) for q in range(4)]

    near = {1: move(at_plane(1, 0), 0, NEAR + 1), 3: move(at_plane(3, 0), 0, NEAR + 3)}
    near[2] = [plain(live(NEAR + (3 if q % 2 else 1), q), live(NEAR + 2, q), at_plane(3 if q % 2 else 1, 0)) for q in range(4)]
    far = {3: move(at_band(3), 0, FAR + 3)}
    relay_at, via_at, far_at = count[0], count[0] + 4, count[0] + 8
    count[0] += 12
    relay = [across(live(VIA, q), live(FAR + 1, q), relay_at + q, far_at + q, at_chip(1, 0)) for q in range(2)]
    relayed = [across(live(VIA, q), live(VIA, q), via_at + q, via_at + q, at_chip(0, 1)) for q in range(2)]
    far[1] = [across(live(0, q), live(FAR + 1, q), far_at + q, far_at + q, at_band(1)) for q in range(4)]
    onward = [
        across(live(0, q), live(jnp.where(is_wrap, VIA, FAR + 1), q), far_at + q, jnp.where(is_wrap, via_at, far_at) + q, next_target)
        for q in range(2)
    ] + far[1][2:]
    skip_target = (jnp.where(is_head, at_chip(1, 1)[0], at_band(1)[0]), plane)
    from_lower = {
        0: plain(live(jnp.where(is_head, VIA, FAR + 1), 0), live(FAR + 2, 0), skip_target),
        2: across(live(FAR + 1, 2), live(FAR + 2, 2), count[0], count[0], at_band(1)),
    }
    from_upper = {2: across(live(FAR + 3, 2), live(FAR + 2, 2), count[0], count[0], at_band(-1))}
    count[0] += 1
    for q in (1, 3):
        from_upper[q] = plain(live(FAR + 3, q), live(FAR + 2, q), at_band(-1))
    far[2] = [(from_upper if q % 2 else from_lower)[q] for q in range(4)]
    sib = {
        t: [plain(grids.at[FAR + t if t else 0, h, :ROWS], grids.at[SIB + t, h, :ROWS], at_plane(0, 1)) for h in range(2)]
        for t in range(4)
    }

    stick_lane = lax.broadcasted_iota(jnp.int32, (HALF, FULL), 1).astype(F32)
    lane = lax.broadcasted_iota(jnp.int32, (FULL, HALF), 1)
    for h in range(2):
        phi = jnp.zeros((FULL, HALF), F32)
        for position, dy in enumerate((0, 1, 3, 2)):
            for flip in range(2):
                if (dy, flip) != (0, 0):
                    chunk_copies[dy * 2 + flip, h].wait_recv()
            rows = jnp.concatenate([got_ref[dy * 2, h], got_ref[dy * 2 + 1, h]], 0)
            if h == 0:
                picked = (jnp.broadcast_to(rows[:, TAG : TAG + 1], (HALF, FULL)) == stick_lane).astype(BF16)
                hart = jnp.concatenate([tables[HART_HI], tables[HART_LO]], 0)
                stick_ref[position] = mm_t(hart, picked).astype(BF16)
            hi, lo = split(rows)
            full = mm(stick_ref[position], jnp.concatenate([hi, lo], 1))
            full = full[:FULL] + full[FULL:]
            phi += full[:, :HALF] + full[:, HALF:]
        if h == 0:
            phi = jnp.where(lane < TAG, phi, 0.0)
        grids[0, h] = phi
        for first, second in ((2 * h, 2 * h + 1), (2 * h + 1, 2 * h)):
            near[1][first].start()
            onward[first].start()
            near[3][second].start()
            far[3][second].start()
        sib[0][h].start()

    back = {
        1: [plain(piece(fields, 1, q), piece(others, 0, q), at_plane(3, 0)) for q in range(4)],
        3: [plain(piece(fields, 3, q), piece(others, 1, q), at_plane(1, 0)) for q in range(4)],
        2: [plain(piece(fields, 2, q), piece(others, 2, q), at_plane(3 if q < 2 else 1, 0)) for q in range(4)],
    }

    for n in range(4):
        fields[n] = jnp.zeros((2, FULL, HALF), F32)
    loads[3].wait()
    loads[4].wait()

    def received(parts):
        for part in parts:
            part.wait_recv()

    def started(parts):
        for part in parts:
            part.start()

    def from_below(q):
        near[1][q].wait_recv()
        near[2][q].start()

        @pl.when(is_head)
        def _():
            if q == 0:
                relayed[0].wait_recv()
                relay[0].start()
                from_lower[0].start()

        @pl.when(jnp.logical_not(is_head))
        def _():
            far[1][q].wait_recv()
            from_lower[q].start()

    def from_above(q):
        near[3][q].wait_recv()
        near[2][q].start()
        far[3][q].wait_recv()
        from_upper[q].start()

        @pl.when(is_head)
        def _():
            if q == 1:
                relayed[1].wait_recv()
                relay[1].start()

        @pl.when(x == 2)
        def _():
            if q == 3:
                far[3][2].wait_recv()
                from_upper[2].start()

    def share(h):
        if h == 0:
            far[3][0].wait_recv()
        else:
            pl.when(x != 2)(far[3][2].wait_recv)
        sib[3][h].start()

        @pl.when(jnp.logical_not(is_head))
        def _():
            far[1][2 * h + 1].wait_recv()
            sib[1][h].start()

    def share_late(h):
        @pl.when(is_head)
        def _():
            received(far[1][2 * h : 2 * h + 2])
            sib[1][h].start()

        received(far[2][2 * h : 2 * h + 2])
        sib[2][h].start()

    def before_0():
        from_below(0)
        from_above(1)
        share(0)
        from_below(2)
        from_above(3)
        share(1)
        received((near[1][1], near[1][3], near[3][0], near[3][2]))
        received(sib[0])

    def before_1():
        received(sib[3])

    def before_2():
        share_late(0)
        received(near[2])

    def before_3():
        share_late(1)
        received(sib[1])

    def before_4():
        received(sib[2])

    def after_4():
        started(back[2])

    def after_5():
        started(back[1][2:])
        started(back[3][:2])

    def merge(n, q):
        back[2][q].wait_recv()
        piece(fields, n, q)[...] += piece(others, 2, q)[...]
        back[n][q].start()

    def after_7():
        for q in range(2):
            merge(1, q)
            merge(3, 2 + q)

    before = {0: before_0, 1: before_1, 2: before_2, 3: before_3, 4: before_4}
    after = {4: after_4, 5: after_5, 7: after_7}

    def body(step, carry):
        for k, action in before.items():
            pl.when(step == k)(action)
        pairs, places = [], []
        for part in range(2):
            n = pick(step, [s[part][0] for s in STEPS])
            t = pick(step, [s[part][1] for s in STEPS])
            own = [grids[n, h] for h in range(2)]
            for g in (jnp.where(t == 0, 0, FAR + t), SIB + t):
                pairs.append((own, [grids[g, h] for h in range(2)]))
            places.append(n)
        values = potentials(pairs, tables, coulomb_ref)
        for part, n in enumerate(places):
            for h in range(2):
                first, second = 2 * part, 2 * part + 1
                fields[n, h] += values[first][h] * pairs[first][1][h] + values[second][h] * pairs[second][1][h]
        for k, action in after.items():
            pl.when(step == k)(action)
        return carry

    lax.fori_loop(0, len(STEPS), body, 0)

    received(back[1])
    received(back[3])
    halves = []
    for h in range(2):
        half = fields[0, h, :ROWS] + others[0, h, :ROWS] + others[1, h, :ROWS]
        halves.append(jnp.concatenate([half, jnp.zeros((FULL - ROWS, HALF), F32)], 0))
    hi, lo = split(jnp.concatenate(halves, 1))
    ordered = mm_t(tables[PLACE_T], hi) + mm_t(tables[PLACE_T], lo)
    hi, lo = split(ordered)
    ordered = mm(hi, tables[PLACE]) + mm(lo, tables[PLACE])
    out_ref[0] = ordered[:N, :N]

    def sent(parts):
        for part in parts:
            part.wait_send()

    sent(onward)
    pl.when(is_head)(functools.partial(sent, relay))
    pl.when(jnp.logical_not(is_head))(from_lower[2].wait_send)
    pl.when(x == 2)(from_upper[2].wait_send)
    for copy in copies:
        copy.wait_send()


def on_device(stick_coef, stick_list):
    tables, coulomb = make_tables()
    tables = jnp.asarray(tables.reshape(10, FULL, FULL))
    dma = pltpu.SemaphoreType.DMA
    return pl.pallas_call(
        kernel,
        out_shape=jax.ShapeDtypeStruct((1, N, N), F32),
        in_specs=[pl.BlockSpec(memory_space=pltpu.HBM)] * 4,
        out_specs=pl.BlockSpec(memory_space=pltpu.VMEM),
        scratch_shapes=[
            pltpu.VMEM((SLOTS, BANDS * N), F32),
            pltpu.VMEM((1, SLOTS), jnp.int32),
            pltpu.VMEM((10, FULL, FULL), BF16),
            pltpu.VMEM((FULL, FULL), F32),
            pltpu.VMEM((BANDS, 2, CHUNK, HALF), F32),
            pltpu.VMEM((BANDS, 2, CHUNK, HALF), F32),
            pltpu.VMEM((4, 2 * FULL, HALF), BF16),
            pltpu.VMEM((VIA + 1, 2, FULL, HALF), F32),
            pltpu.VMEM((4, 2, FULL, HALF), F32),
            pltpu.VMEM((3, 2, FULL, HALF), F32),
            dma((5,)),
            dma((84,)),
            dma((84,)),
        ],
        compiler_params=pltpu.CompilerParams(
            collective_id=0, has_side_effects=True, vmem_limit_bytes=40 * 1024 * 1024
        ),
    )(*(pltpu.with_memory_space_constraint(v, pltpu.HBM) for v in (stick_coef, stick_list.reshape(1, SLOTS), tables, jnp.asarray(coulomb))))


def solution(mesh):
    in_specs = (P("plane", "band"), P("plane"))
    out_specs = P(("band", "plane"), None, None)
    return jax.shard_map(on_device, mesh=mesh, in_specs=in_specs, out_specs=out_specs, check_vma=False)
```

```python
import functools
import math

import jax
import jax.numpy as jnp
import ml_dtypes
import numpy as np
from jax import lax
from jax.experimental import pallas as pl
from jax.experimental.pallas import tpu as pltpu
from jax.sharding import PartitionSpec as P

N = 240
HALF = 128
FULL = 256
ROWS = 248
SLOTS = 60
CHUNK = 64
BANDS = 8
MESH = pl.DeviceIdType.MESH
F32 = jnp.float32
BF16 = jnp.bfloat16


def split_np(values):
    high = values.astype(np.float32).astype(ml_dtypes.bfloat16)
    low = (values - high.astype(np.float64)).astype(np.float32).astype(ml_dtypes.bfloat16)
    return high, low


def make_tables():
    spot = -np.ones(FULL, np.int64)
    spot[:121] = np.arange(121)
    spot[HALF + 1 : HALF + 120] = N - np.arange(1, 120)
    index = np.arange(N)
    phase = (index[:, None] * index[None, :] % N) * (2.0 * np.pi / N)
    hart = (np.cos(phase) + np.sin(phase)) / math.sqrt(N)
    folded = np.zeros((FULL, FULL))
    folded[spot >= 0, :N] = hart[spot[spot >= 0]]
    f_hi, f_lo = split_np(folded)
    cosine = np.zeros((HALF, HALF))
    cosine[:121, :121] = np.cos(phase[:121, :121]) / math.sqrt(N)
    sine = np.zeros((HALF, HALF))
    sine[1:120, 1:120] = np.sin(phase[1:120, 1:120]) / math.sqrt(N)
    right, left = [], []
    for table in (cosine, sine):
        hi, lo = split_np(table)
        right.append(np.block([[hi, lo], [hi, lo]]))
        left.append(np.block([[hi, hi], [lo, lo]]))
    freq = np.arange(HALF).astype(np.float64)
    weight = np.where((freq == 0) | (freq == 120), 1.0, 2.0)
    squared = freq[:, None] ** 2 + freq[None, :] ** 2
    coulomb = np.where(squared > 0, 0.25 * N / np.maximum(squared, 1.0), 0.0)
    coulomb = coulomb * weight[:, None] * weight[None, :]
    even = (freq <= 120).astype(np.float64)
    odd = ((freq >= 1) & (freq <= 119)).astype(np.float64)
    live = np.concatenate([even, odd])
    coulomb = (np.tile(coulomb, (2, 2)) * live[:, None] * live[None, :]).astype(np.float32)
    place = np.zeros((FULL, FULL), np.float32)
    for p in range(FULL):
        if spot[p] >= 0:
            place[p, spot[p]] = 1.0
    bf16 = ml_dtypes.bfloat16
    blocks = [f_hi.T, f_lo.T, f_hi, f_lo, *right, *left, place.astype(bf16), place.T.astype(bf16)]
    return np.concatenate(blocks, 0), coulomb


def split(values):
    high = values.astype(BF16)
    low = (values - high.astype(F32)).astype(BF16)
    return high, low


def mm(lhs, rhs):
    return lax.dot_general(lhs, rhs, (((1,), (0,)), ((), ())), preferred_element_type=F32)


def mm_t(lhs, rhs):
    return lax.dot_general(lhs, rhs, (((1,), (1,)), ((), ())), preferred_element_type=F32)


def along_lanes(halves, tables):
    out = []
    for p in range(2):
        hi, lo = split(halves[p])
        full = mm(jnp.concatenate([hi, lo], 1), tables[RIGHT + p])
        out.append(full[:, :HALF] + full[:, HALF:])
    return out


def along_rows(halves, tables):
    out = []
    for p in range(2):
        hi, lo = split(halves[p])
        full = mm(tables[LEFT + p], jnp.concatenate([hi, lo], 0))
        out.append(full[:HALF] + full[HALF:])
    return out


def to_rows(pair):
    return [jnp.concatenate([pair[0][k * HALF : (k + 1) * HALF], pair[1][k * HALF : (k + 1) * HALF]], 1) for k in range(2)]


def to_lanes(pair):
    return [jnp.concatenate([pair[0][:, k * HALF : (k + 1) * HALF], pair[1][:, k * HALF : (k + 1) * HALF]], 0) for k in range(2)]


def fold_rows(values):
    return jnp.concatenate([values[:HALF] + values[HALF:], values[:HALF] - values[HALF:]], 0)


def potentials(pairs, tables, coulomb_ref):
    states = []
    for own, partner in pairs:
        plus, minus = own[0] * partner[0], own[1] * partner[1]
        states.append([fold_rows(plus + minus), fold_rows(plus - minus)])
    states = [to_rows(along_lanes(s, tables)) for s in states]
    states = [along_rows(s, tables) for s in states]
    states = [[s[k] * coulomb_ref[k * HALF : (k + 1) * HALF] for k in range(2)] for s in states]
    states = [to_lanes(along_rows(s, tables)) for s in states]
    states = [along_lanes(s, tables) for s in states]
    return [[fold_rows(even + odd), fold_rows(even - odd)] for even, odd in states]


BACK_HI, BACK_LO, HART_HI, HART_LO, RIGHT, LEFT, PLACE, PLACE_T = 0, 1, 2, 3, 4, 6, 8, 9
TAG = 121
NEAR, FAR, SIB, VIA = 0, 3, 7, 11

STEPS = (
    ((1, 0), (3, 0)),
    ((1, 3), (3, 3)),
    ((2, 0), (2, 3)),
    ((1, 1), (3, 1)),
    ((2, 1), (2, 2)),
    ((1, 2), (3, 2)),
    ((0, 0), (0, 3)),
    ((0, 1), (0, 2)),
)


def pick(step, table):
    value = jnp.int32(table[0])
    for position, entry in enumerate(table):
        if position and entry != table[0]:
            value = jnp.where(step == position, jnp.int32(entry), value)
    return value


def kernel(
    coef_hbm, list_hbm, table_hbm, coulomb_hbm, out_ref,
    coef_ref, list_ref, tables, coulomb_ref, send_ref, got_ref, stick_ref, grids, fields, others,
    local_sem, send_sem, recv_sem,
):
    band = lax.axis_index("band")
    plane = lax.axis_index("plane")
    n_band = lax.axis_size("band")
    y, core = plane // 2, plane % 2
    z, x = band // 4, band % 4
    n_z = n_band // 4
    is_head, is_wrap = x == 0, x == 3

    def at_plane(dy, flip):
        return (band, (y + dy) % 4 * 2 + (core + flip) % 2)

    def at_band(t):
        return ((band + t + n_band) % n_band, plane)

    def at_chip(dz, dx):
        return ((z + dz + n_z) % n_z * 4 + (x + dx + 4) % 4, plane)

    next_target = (jnp.where(is_wrap, at_chip(0, 1)[0], at_band(1)[0]), plane)

    barrier = pltpu.get_barrier_semaphore()
    peers = [at_plane(dy, flip) for dy in range(4) for flip in range(2) if (dy, flip) != (0, 0)]
    peers += [at_band(t) for t in (1, 3, -1, -3)]
    peers += [at_chip(0, 1), at_chip(0, -1), at_chip(1, 0), at_chip(-1, 0), at_chip(1, 1), at_chip(-1, -1)]
    for peer in peers:
        pl.semaphore_signal(barrier, inc=1, device_id=peer, device_id_type=MESH)

    loads = [
        pltpu.make_async_copy(list_hbm, list_ref, local_sem.at[0]),
        pltpu.make_async_copy(coef_hbm, coef_ref, local_sem.at[1]),
        pltpu.make_async_copy(table_hbm.at[:4], tables.at[:4], local_sem.at[2]),
        pltpu.make_async_copy(table_hbm.at[4:], tables.at[4:], local_sem.at[3]),
        pltpu.make_async_copy(coulomb_hbm, coulomb_ref, local_sem.at[4]),
    ]
    for load in loads:
        load.start()
    for g in range(VIA + 1):
        for h in range(2):
            grids[g, h, ROWS:, :] = jnp.zeros((FULL - ROWS, HALF), F32)

    lane = lax.broadcasted_iota(jnp.int32, (CHUNK, HALF), 1)
    row = lax.broadcasted_iota(jnp.int32, (CHUNK, HALF), 0)
    loads[0].wait()
    listed = jnp.concatenate([list_ref[...].astype(F32), jnp.full((1, HALF - SLOTS), -1.0, F32)], 1)
    column = jnp.sum(jnp.where(lane == row, jnp.broadcast_to(listed, (CHUNK, HALF)), 0.0), axis=1, keepdims=True)
    tag = jnp.broadcast_to(column, (CHUNK, HALF))
    loads[1].wait()
    loads[2].wait()
    for b in range(BANDS):
        chunk = jnp.concatenate([coef_ref[:, b * N : (b + 1) * N], jnp.zeros((SLOTS, FULL - N), F32)], 1)
        chunk = jnp.concatenate([chunk, jnp.zeros((CHUNK - SLOTS, FULL), F32)], 0)
        hi, lo = split(chunk)
        moved = mm(jnp.concatenate([hi, lo], 0), tables[BACK_HI])
        moved = moved[:CHUNK] + moved[CHUNK:] + mm(hi, tables[BACK_LO])
        send_ref[b, 0] = jnp.where(lane == TAG, tag, moved[:, :HALF])
        send_ref[b, 1] = moved[:, HALF:]
    pl.semaphore_wait(barrier, len(peers))

    count = [0]
    copies = []

    def across(src, dst, send, recv, target):
        return pltpu.make_async_remote_copy(
            src_ref=src, dst_ref=dst, send_sem=send_sem.at[send], recv_sem=recv_sem.at[recv],
            device_id=target, device_id_type=MESH,
        )

    def plain(src, dst, target):
        copies.append(across(src, dst, count[0], count[0], target))
        count[0] += 1
        return copies[-1]

    chunk_copies = {}
    for h in range(2):
        for dy, flip in ((2, 0), (2, 1), (1, 0), (3, 0), (1, 1), (3, 1), (0, 1)):
            target = at_plane(dy, flip)
            slot = dy * 2 + flip
            args = (send_ref.at[target[1], h], got_ref.at[slot, h])
            chunk_copies[slot, h] = across(*args, count[0], count[0], target)
            count[0] += 1
            copies.append(chunk_copies[slot, h])
            chunk_copies[slot, h].start()
    got_ref[0] = send_ref[plane]

    def piece(ref, g, q):
        return ref.at[g, q // 2, pl.ds(q % 2 * HALF, ROWS - HALF if q % 2 else HALF)]

    def live(g, q):
        return piece(grids, g, q)

    def move(target, src, dst):
        return [plain(live(src, q), live(dst, q), target) for q in range(4)]

    near = {1: move(at_plane(1, 0), 0, NEAR + 1), 3: move(at_plane(3, 0), 0, NEAR + 3)}
    near[2] = [plain(live(NEAR + (3 if q % 2 else 1), q), live(NEAR + 2, q), at_plane(3 if q % 2 else 1, 0)) for q in range(4)]
    far = {3: move(at_band(3), 0, FAR + 3)}
    relay_at, via_at, far_at = count[0], count[0] + 4, count[0] + 8
    count[0] += 12
    relay = [across(live(VIA, q), live(FAR + 1, q), relay_at + q, far_at + q, at_chip(1, 0)) for q in range(2)]
    relayed = [across(live(VIA, q), live(VIA, q), via_at + q, via_at + q, at_chip(0, 1)) for q in range(2)]
    far[1] = [across(live(0, q), live(FAR + 1, q), far_at + q, far_at + q, at_band(1)) for q in range(4)]
    onward = [
        across(live(0, q), live(jnp.where(is_wrap, VIA, FAR + 1), q), far_at + q, jnp.where(is_wrap, via_at, far_at) + q, next_target)
        for q in range(2)
    ] + far[1][2:]
    skip_target = (jnp.where(is_head, at_chip(1, 1)[0], at_band(1)[0]), plane)
    from_lower = {
        0: plain(live(jnp.where(is_head, VIA, FAR + 1), 0), live(FAR + 2, 0), skip_target),
        2: across(live(FAR + 1, 2), live(FAR + 2, 2), count[0], count[0], at_band(1)),
    }
    from_upper = {2: across(live(FAR + 3, 2), live(FAR + 2, 2), count[0], count[0], at_band(-1))}
    count[0] += 1
    for q in (1, 3):
        from_upper[q] = plain(live(FAR + 3, q), live(FAR + 2, q), at_band(-1))
    far[2] = [(from_upper if q % 2 else from_lower)[q] for q in range(4)]
    sib = {
        t: [plain(grids.at[FAR + t if t else 0, h, :ROWS], grids.at[SIB + t, h, :ROWS], at_plane(0, 1)) for h in range(2)]
        for t in range(4)
    }

    stick_lane = lax.broadcasted_iota(jnp.int32, (HALF, FULL), 1).astype(F32)
    lane = lax.broadcasted_iota(jnp.int32, (FULL, HALF), 1)
    for h in range(2):
        phi = jnp.zeros((FULL, HALF), F32)
        for position, dy in enumerate((0, 1, 3, 2)):
            for flip in range(2):
                if (dy, flip) != (0, 0):
                    chunk_copies[dy * 2 + flip, h].wait_recv()
            rows = jnp.concatenate([got_ref[dy * 2, h], got_ref[dy * 2 + 1, h]], 0)
            if h == 0:
                picked = (jnp.broadcast_to(rows[:, TAG : TAG + 1], (HALF, FULL)) == stick_lane).astype(BF16)
                hart = jnp.concatenate([tables[HART_HI], tables[HART_LO]], 0)
                stick_ref[position] = mm_t(hart, picked).astype(BF16)
            hi, lo = split(rows)
            full = mm(stick_ref[position], jnp.concatenate([hi, lo], 1))
            full = full[:FULL] + full[FULL:]
            phi += full[:, :HALF] + full[:, HALF:]
        if h == 0:
            phi = jnp.where(lane < TAG, phi, 0.0)
        grids[0, h] = phi
        for first, second in ((2 * h, 2 * h + 1), (2 * h + 1, 2 * h)):
            near[1][first].start()
            onward[first].start()
            near[3][second].start()
            far[3][second].start()
        sib[0][h].start()

    back = {
        1: [plain(piece(fields, 1, q), piece(others, 0, q), at_plane(3, 0)) for q in range(4)],
        3: [plain(piece(fields, 3, q), piece(others, 1, q), at_plane(1, 0)) for q in range(4)],
        2: [plain(piece(fields, 2, q), piece(others, 2, q), at_plane(3 if q < 2 else 1, 0)) for q in range(4)],
    }

    for n in range(4):
        fields[n] = jnp.zeros((2, FULL, HALF), F32)
    loads[3].wait()
    loads[4].wait()

    def received(parts):
        for part in parts:
            part.wait_recv()

    def started(parts):
        for part in parts:
            part.start()

    def from_below(q):
        near[1][q].wait_recv()
        near[2][q].start()

        @pl.when(is_head)
        def _():
            if q == 0:
                relayed[0].wait_recv()
                relay[0].start()
                from_lower[0].start()

        @pl.when(jnp.logical_not(is_head))
        def _():
            far[1][q].wait_recv()
            from_lower[q].start()

    def from_above(q):
        near[3][q].wait_recv()
        near[2][q].start()
        far[3][q].wait_recv()
        from_upper[q].start()

        @pl.when(is_head)
        def _():
            if q == 1:
                relayed[1].wait_recv()
                relay[1].start()

        @pl.when(x == 2)
        def _():
            if q == 3:
                far[3][2].wait_recv()
                from_upper[2].start()

    def share(h):
        if h == 0:
            far[3][0].wait_recv()
        else:
            pl.when(x != 2)(far[3][2].wait_recv)
        sib[3][h].start()

        @pl.when(jnp.logical_not(is_head))
        def _():
            far[1][2 * h + 1].wait_recv()
            sib[1][h].start()

    def share_late(h):
        @pl.when(is_head)
        def _():
            received(far[1][2 * h : 2 * h + 2])
            sib[1][h].start()

        received(far[2][2 * h : 2 * h + 2])
        sib[2][h].start()

    def before_0():
        from_below(0)
        from_above(1)
        share(0)
        from_below(2)
        from_above(3)
        share(1)
        received((near[1][1], near[1][3], near[3][0], near[3][2]))
        received(sib[0])

    def before_1():
        received(sib[3])

    def before_2():
        share_late(0)
        received(near[2])

    def before_3():
        share_late(1)
        received(sib[1])

    def before_4():
        received(sib[2])

    def after_4():
        started(back[2])

    def after_5():
        started(back[1][2:])
        started(back[3][:2])

    def merge(n, q):
        back[2][q].wait_recv()
        piece(fields, n, q)[...] += piece(others, 2, q)[...]
        back[n][q].start()

    def after_7():
        for q in range(2):
            merge(1, q)
            merge(3, 2 + q)

    before = {0: before_0, 1: before_1, 2: before_2, 3: before_3, 4: before_4}
    after = {4: after_4, 5: after_5, 7: after_7}

    def body(step, carry):
        for k, action in before.items():
            pl.when(step == k)(action)
        pairs, places = [], []
        for part in range(2):
            n = pick(step, [s[part][0] for s in STEPS])
            t = pick(step, [s[part][1] for s in STEPS])
            own = [grids[n, h] for h in range(2)]
            for g in (jnp.where(t == 0, 0, FAR + t), SIB + t):
                pairs.append((own, [grids[g, h] for h in range(2)]))
            places.append(n)
        values = potentials(pairs, tables, coulomb_ref)
        for part, n in enumerate(places):
            for h in range(2):
                first, second = 2 * part, 2 * part + 1
                fields[n, h] += values[first][h] * pairs[first][1][h] + values[second][h] * pairs[second][1][h]
        for k, action in after.items():
            pl.when(step == k)(action)
        return carry

    lax.fori_loop(0, len(STEPS), body, 0)

    received(back[1])
    received(back[3])
    halves = []
    for h in range(2):
        half = fields[0, h, :ROWS] + others[0, h, :ROWS] + others[1, h, :ROWS]
        halves.append(jnp.concatenate([half, jnp.zeros((FULL - ROWS, HALF), F32)], 0))
    hi, lo = split(jnp.concatenate(halves, 1))
    ordered = mm_t(tables[PLACE_T], hi) + mm_t(tables[PLACE_T], lo)
    hi, lo = split(ordered)
    ordered = mm(hi, tables[PLACE]) + mm(lo, tables[PLACE])
    out_ref[0] = ordered[:N, :N]

    def sent(parts):
        for part in parts:
            part.wait_send()

    sent(onward)
    pl.when(is_head)(functools.partial(sent, relay))
    pl.when(jnp.logical_not(is_head))(from_lower[2].wait_send)
    pl.when(x == 2)(from_upper[2].wait_send)
    for copy in copies:
        copy.wait_send()


def on_device(stick_coef, stick_list):
    tables, coulomb = make_tables()
    tables = jnp.asarray(tables.reshape(10, FULL, FULL))
    dma = pltpu.SemaphoreType.DMA
    return pl.pallas_call(
        kernel,
        out_shape=jax.ShapeDtypeStruct((1, N, N), F32),
        in_specs=[pl.BlockSpec(memory_space=pltpu.HBM)] * 4,
        out_specs=pl.BlockSpec(memory_space=pltpu.VMEM),
        scratch_shapes=[
            pltpu.VMEM((SLOTS, BANDS * N), F32),
            pltpu.VMEM((1, SLOTS), jnp.int32),
            pltpu.VMEM((10, FULL, FULL), BF16),
            pltpu.VMEM((FULL, FULL), F32),
            pltpu.VMEM((BANDS, 2, CHUNK, HALF), F32),
            pltpu.VMEM((BANDS, 2, CHUNK, HALF), F32),
            pltpu.VMEM((4, 2 * FULL, HALF), BF16),
            pltpu.VMEM((VIA + 1, 2, FULL, HALF), F32),
            pltpu.VMEM((4, 2, FULL, HALF), F32),
            pltpu.VMEM((3, 2, FULL, HALF), F32),
            dma((5,)),
            dma((84,)),
            dma((84,)),
        ],
        compiler_params=pltpu.CompilerParams(
            collective_id=0, has_side_effects=True, vmem_limit_bytes=40 * 1024 * 1024
        ),
    )(*(pltpu.with_memory_space_constraint(v, pltpu.HBM) for v in (stick_coef, stick_list.reshape(1, SLOTS), tables, jnp.asarray(coulomb))))


def solution(mesh):
    in_specs = (P("plane", "band"), P("plane"))
    out_specs = P(("band", "plane"), None, None)
    return jax.shard_map(on_device, mesh=mesh, in_specs=in_specs, out_specs=out_specs, check_vma=False)
```

```python
import functools
import math

import jax
import jax.numpy as jnp
import ml_dtypes
import numpy as np
from jax import lax
from jax.experimental import pallas as pl
from jax.experimental.pallas import tpu as pltpu
from jax.sharding import PartitionSpec as P

N = 240
HALF = 128
FULL = 256
ROWS = 248
SLOTS = 60
CHUNK = 64
BANDS = 8
MESH = pl.DeviceIdType.MESH
F32 = jnp.float32
BF16 = jnp.bfloat16


def split_np(values):
    high = values.astype(np.float32).astype(ml_dtypes.bfloat16)
    low = (values - high.astype(np.float64)).astype(np.float32).astype(ml_dtypes.bfloat16)
    return high, low


def make_tables():
    spot = -np.ones(FULL, np.int64)
    spot[:121] = np.arange(121)
    spot[HALF + 1 : HALF + 120] = N - np.arange(1, 120)
    index = np.arange(N)
    phase = (index[:, None] * index[None, :] % N) * (2.0 * np.pi / N)
    hart = (np.cos(phase) + np.sin(phase)) / math.sqrt(N)
    folded = np.zeros((FULL, FULL))
    folded[spot >= 0, :N] = hart[spot[spot >= 0]]
    f_hi, f_lo = split_np(folded)
    cosine = np.zeros((HALF, HALF))
    cosine[:121, :121] = np.cos(phase[:121, :121]) / math.sqrt(N)
    sine = np.zeros((HALF, HALF))
    sine[1:120, 1:120] = np.sin(phase[1:120, 1:120]) / math.sqrt(N)
    right, left = [], []
    for table in (cosine, sine):
        hi, lo = split_np(table)
        right.append(np.block([[hi, lo], [hi, lo]]))
        left.append(np.block([[hi, hi], [lo, lo]]))
    freq = np.arange(HALF).astype(np.float64)
    weight = np.where((freq == 0) | (freq == 120), 1.0, 2.0)
    squared = freq[:, None] ** 2 + freq[None, :] ** 2
    coulomb = np.where(squared > 0, 0.25 * N / np.maximum(squared, 1.0), 0.0)
    coulomb = coulomb * weight[:, None] * weight[None, :]
    even = (freq <= 120).astype(np.float64)
    odd = ((freq >= 1) & (freq <= 119)).astype(np.float64)
    live = np.concatenate([even, odd])
    coulomb = (np.tile(coulomb, (2, 2)) * live[:, None] * live[None, :]).astype(np.float32)
    place = np.zeros((FULL, FULL), np.float32)
    for p in range(FULL):
        if spot[p] >= 0:
            place[p, spot[p]] = 1.0
    bf16 = ml_dtypes.bfloat16
    blocks = [f_hi.T, f_lo.T, f_hi, f_lo, *right, *left, place.astype(bf16), place.T.astype(bf16)]
    return np.concatenate(blocks, 0), coulomb


def split(values):
    high = values.astype(BF16)
    low = (values - high.astype(F32)).astype(BF16)
    return high, low


def mm(lhs, rhs):
    return lax.dot_general(lhs, rhs, (((1,), (0,)), ((), ())), preferred_element_type=F32)


def mm_t(lhs, rhs):
    return lax.dot_general(lhs, rhs, (((1,), (1,)), ((), ())), preferred_element_type=F32)


def along_lanes(halves, tables):
    out = []
    for p in range(2):
        hi, lo = split(halves[p])
        full = mm(jnp.concatenate([hi, lo], 1), tables[RIGHT + p])
        out.append(full[:, :HALF] + full[:, HALF:])
    return out


def along_rows(halves, tables):
    out = []
    for p in range(2):
        hi, lo = split(halves[p])
        full = mm(tables[LEFT + p], jnp.concatenate([hi, lo], 0))
        out.append(full[:HALF] + full[HALF:])
    return out


def to_rows(pair):
    return [jnp.concatenate([pair[0][k * HALF : (k + 1) * HALF], pair[1][k * HALF : (k + 1) * HALF]], 1) for k in range(2)]


def to_lanes(pair):
    return [jnp.concatenate([pair[0][:, k * HALF : (k + 1) * HALF], pair[1][:, k * HALF : (k + 1) * HALF]], 0) for k in range(2)]


def fold_rows(values):
    return jnp.concatenate([values[:HALF] + values[HALF:], values[:HALF] - values[HALF:]], 0)


def potentials(pairs, tables, coulomb_ref):
    states = []
    for own, partner in pairs:
        plus, minus = own[0] * partner[0], own[1] * partner[1]
        states.append([fold_rows(plus + minus), fold_rows(plus - minus)])
    states = [to_rows(along_lanes(s, tables)) for s in states]
    states = [along_rows(s, tables) for s in states]
    states = [[s[k] * coulomb_ref[k * HALF : (k + 1) * HALF] for k in range(2)] for s in states]
    states = [to_lanes(along_rows(s, tables)) for s in states]
    states = [along_lanes(s, tables) for s in states]
    return [[fold_rows(even + odd), fold_rows(even - odd)] for even, odd in states]


BACK_HI, BACK_LO, HART_HI, HART_LO, RIGHT, LEFT, PLACE, PLACE_T = 0, 1, 2, 3, 4, 6, 8, 9
TAG = 121
NEAR, FAR, SIB, VIA = 0, 3, 7, 11

STEPS = (
    ((1, 0), (3, 0)),
    ((1, 3), (3, 3)),
    ((2, 0), (2, 3)),
    ((1, 1), (3, 1)),
    ((2, 1), (2, 2)),
    ((1, 2), (3, 2)),
    ((0, 0), (0, 3)),
    ((0, 1), (0, 2)),
)


def pick(step, table):
    value = jnp.int32(table[0])
    for position, entry in enumerate(table):
        if position and entry != table[0]:
            value = jnp.where(step == position, jnp.int32(entry), value)
    return value


def kernel(
    coef_hbm, list_hbm, table_hbm, coulomb_hbm, out_ref,
    coef_ref, list_ref, tables, coulomb_ref, send_ref, got_ref, stick_ref, grids, fields, others,
    local_sem, send_sem, recv_sem,
):
    band = lax.axis_index("band")
    plane = lax.axis_index("plane")
    n_band = lax.axis_size("band")
    y, core = plane // 2, plane % 2
    z, x = band // 4, band % 4
    n_z = n_band // 4
    is_head, is_wrap = x == 0, x == 3

    def at_plane(dy, flip):
        return (band, (y + dy) % 4 * 2 + (core + flip) % 2)

    def at_band(t):
        return ((band + t + n_band) % n_band, plane)

    def at_chip(dz, dx):
        return ((z + dz + n_z) % n_z * 4 + (x + dx + 4) % 4, plane)

    next_target = (jnp.where(is_wrap, at_chip(0, 1)[0], at_band(1)[0]), plane)

    barrier = pltpu.get_barrier_semaphore()
    peers = [at_plane(dy, flip) for dy in range(4) for flip in range(2) if (dy, flip) != (0, 0)]
    peers += [at_band(t) for t in (1, 3, -1, -3)]
    peers += [at_chip(0, 1), at_chip(0, -1), at_chip(1, 0), at_chip(-1, 0), at_chip(1, 1), at_chip(-1, -1)]
    for peer in peers:
        pl.semaphore_signal(barrier, inc=1, device_id=peer, device_id_type=MESH)

    loads = [
        pltpu.make_async_copy(list_hbm, list_ref, local_sem.at[0]),
        pltpu.make_async_copy(coef_hbm, coef_ref, local_sem.at[1]),
        pltpu.make_async_copy(table_hbm.at[:4], tables.at[:4], local_sem.at[2]),
        pltpu.make_async_copy(table_hbm.at[4:], tables.at[4:], local_sem.at[3]),
        pltpu.make_async_copy(coulomb_hbm, coulomb_ref, local_sem.at[4]),
    ]
    for load in loads:
        load.start()
    for g in range(VIA + 1):
        for h in range(2):
            grids[g, h, ROWS:, :] = jnp.zeros((FULL - ROWS, HALF), F32)

    lane = lax.broadcasted_iota(jnp.int32, (CHUNK, HALF), 1)
    row = lax.broadcasted_iota(jnp.int32, (CHUNK, HALF), 0)
    loads[0].wait()
    listed = jnp.concatenate([list_ref[...].astype(F32), jnp.full((1, HALF - SLOTS), -1.0, F32)], 1)
    column = jnp.sum(jnp.where(lane == row, jnp.broadcast_to(listed, (CHUNK, HALF)), 0.0), axis=1, keepdims=True)
    tag = jnp.broadcast_to(column, (CHUNK, HALF))
    loads[1].wait()
    loads[2].wait()
    for b in range(BANDS):
        chunk = jnp.concatenate([coef_ref[:, b * N : (b + 1) * N], jnp.zeros((SLOTS, FULL - N), F32)], 1)
        chunk = jnp.concatenate([chunk, jnp.zeros((CHUNK - SLOTS, FULL), F32)], 0)
        hi, lo = split(chunk)
        moved = mm(jnp.concatenate([hi, lo], 0), tables[BACK_HI])
        moved = moved[:CHUNK] + moved[CHUNK:] + mm(hi, tables[BACK_LO])
        send_ref[b, 0] = jnp.where(lane == TAG, tag, moved[:, :HALF])
        send_ref[b, 1] = moved[:, HALF:]
    pl.semaphore_wait(barrier, len(peers))

    count = [0]
    copies = []

    def across(src, dst, send, recv, target):
        return pltpu.make_async_remote_copy(
            src_ref=src, dst_ref=dst, send_sem=send_sem.at[send], recv_sem=recv_sem.at[recv],
            device_id=target, device_id_type=MESH,
        )

    def plain(src, dst, target):
        copies.append(across(src, dst, count[0], count[0], target))
        count[0] += 1
        return copies[-1]

    chunk_copies = {}
    for h in range(2):
        for dy, flip in ((2, 0), (2, 1), (1, 0), (3, 0), (1, 1), (3, 1), (0, 1)):
            target = at_plane(dy, flip)
            slot = dy * 2 + flip
            args = (send_ref.at[target[1], h], got_ref.at[slot, h])
            chunk_copies[slot, h] = across(*args, count[0], count[0], target)
            count[0] += 1
            copies.append(chunk_copies[slot, h])
            chunk_copies[slot, h].start()
    got_ref[0] = send_ref[plane]

    def piece(ref, g, q):
        return ref.at[g, q // 2, pl.ds(q % 2 * HALF, ROWS - HALF if q % 2 else HALF)]

    def live(g, q):
        return piece(grids, g, q)

    def move(target, src, dst):
        return [plain(live(src, q), live(dst, q), target) for q in range(4)]

    near = {1: move(at_plane(1, 0), 0, NEAR + 1), 3: move(at_plane(3, 0), 0, NEAR + 3)}
    near[2] = [plain(live(NEAR + (3 if q % 2 else 1), q), live(NEAR + 2, q), at_plane(3 if q % 2 else 1, 0)) for q in range(4)]
    far = {3: move(at_band(3), 0, FAR + 3)}
    relay_at, via_at, far_at = count[0], count[0] + 4, count[0] + 8
    count[0] += 12
    relay = [across(live(VIA, q), live(FAR + 1, q), relay_at + q, far_at + q, at_chip(1, 0)) for q in range(2)]
    relayed = [across(live(VIA, q), live(VIA, q), via_at + q, via_at + q, at_chip(0, 1)) for q in range(2)]
    far[1] = [across(live(0, q), live(FAR + 1, q), far_at + q, far_at + q, at_band(1)) for q in range(4)]
    onward = [
        across(live(0, q), live(jnp.where(is_wrap, VIA, FAR + 1), q), far_at + q, jnp.where(is_wrap, via_at, far_at) + q, next_target)
        for q in range(2)
    ] + far[1][2:]
    skip_target = (jnp.where(is_head, at_chip(1, 1)[0], at_band(1)[0]), plane)
    from_lower = {
        0: plain(live(jnp.where(is_head, VIA, FAR + 1), 0), live(FAR + 2, 0), skip_target),
        2: across(live(FAR + 1, 2), live(FAR + 2, 2), count[0], count[0], at_band(1)),
    }
    from_upper = {2: across(live(FAR + 3, 2), live(FAR + 2, 2), count[0], count[0], at_band(-1))}
    count[0] += 1
    for q in (1, 3):
        from_upper[q] = plain(live(FAR + 3, q), live(FAR + 2, q), at_band(-1))
    far[2] = [(from_upper if q % 2 else from_lower)[q] for q in range(4)]
    sib = {
        t: [plain(grids.at[FAR + t if t else 0, h, :ROWS], grids.at[SIB + t, h, :ROWS], at_plane(0, 1)) for h in range(2)]
        for t in range(4)
    }

    stick_lane = lax.broadcasted_iota(jnp.int32, (HALF, FULL), 1).astype(F32)
    lane = lax.broadcasted_iota(jnp.int32, (FULL, HALF), 1)
    for h in range(2):
        phi = jnp.zeros((FULL, HALF), F32)
        for position, dy in enumerate((0, 1, 3, 2)):
            for flip in range(2):
                if (dy, flip) != (0, 0):
                    chunk_copies[dy * 2 + flip, h].wait_recv()
            rows = jnp.concatenate([got_ref[dy * 2, h], got_ref[dy * 2 + 1, h]], 0)
            if h == 0:
                picked = (jnp.broadcast_to(rows[:, TAG : TAG + 1], (HALF, FULL)) == stick_lane).astype(BF16)
                hart = jnp.concatenate([tables[HART_HI], tables[HART_LO]], 0)
                stick_ref[position] = mm_t(hart, picked).astype(BF16)
            hi, lo = split(rows)
            full = mm(stick_ref[position], jnp.concatenate([hi, lo], 1))
            full = full[:FULL] + full[FULL:]
            phi += full[:, :HALF] + full[:, HALF:]
        if h == 0:
            phi = jnp.where(lane < TAG, phi, 0.0)
        grids[0, h] = phi
        for first, second in ((2 * h, 2 * h + 1), (2 * h + 1, 2 * h)):
            near[1][first].start()
            onward[first].start()
            near[3][second].start()
            far[3][second].start()
        sib[0][h].start()

    back = {
        1: [plain(piece(fields, 1, q), piece(others, 0, q), at_plane(3, 0)) for q in range(4)],
        3: [plain(piece(fields, 3, q), piece(others, 1, q), at_plane(1, 0)) for q in range(4)],
        2: [plain(piece(fields, 2, q), piece(others, 2, q), at_plane(3 if q < 2 else 1, 0)) for q in range(4)],
    }

    for n in range(4):
        fields[n] = jnp.zeros((2, FULL, HALF), F32)
    loads[3].wait()
    loads[4].wait()

    def received(parts):
        for part in parts:
            part.wait_recv()

    def started(parts):
        for part in parts:
            part.start()

    def pass_near(q):
        near[3 if q % 2 else 1][q].wait_recv()
        near[2][q].start()

    def from_below(q):
        @pl.when(is_head)
        def _():
            if q == 0:
                relayed[0].wait_recv()
                relay[0].start()
                from_lower[0].start()

        @pl.when(jnp.logical_not(is_head))
        def _():
            far[1][q].wait_recv()
            from_lower[q].start()

    def from_above(q):
        far[3][q].wait_recv()
        from_upper[q].start()

        @pl.when(is_head)
        def _():
            if q == 1:
                relayed[1].wait_recv()
                relay[1].start()

        @pl.when(x == 2)
        def _():
            if q == 3:
                far[3][2].wait_recv()
                from_upper[2].start()

    def share(h):
        if h == 0:
            far[3][0].wait_recv()
        else:
            pl.when(x != 2)(far[3][2].wait_recv)
        sib[3][h].start()

        @pl.when(jnp.logical_not(is_head))
        def _():
            far[1][2 * h + 1].wait_recv()
            sib[1][h].start()

    def share_late(h):
        @pl.when(is_head)
        def _():
            received(far[1][2 * h : 2 * h + 2])
            sib[1][h].start()

        received(far[2][2 * h : 2 * h + 2])
        sib[2][h].start()

    def before_0():
        from_below(0)
        from_above(1)
        share(0)
        pass_near(0)
        pass_near(1)
        from_below(2)
        from_above(3)
        share(1)
        pass_near(2)
        pass_near(3)
        received((near[1][1], near[1][3], near[3][0], near[3][2]))
        received(sib[0])

    def before_1():
        received(sib[3])

    def before_2():
        share_late(0)
        received(near[2])

    def before_3():
        share_late(1)
        received(sib[1])

    def before_4():
        received(sib[2])

    def after_4():
        started(back[2])

    def after_5():
        started(back[1][2:])
        started(back[3][:2])

    def merge(n, q):
        back[2][q].wait_recv()
        piece(fields, n, q)[...] += piece(others, 2, q)[...]
        back[n][q].start()

    def after_7():
        for q in range(2):
            merge(1, q)
            merge(3, 2 + q)

    before = {0: before_0, 1: before_1, 2: before_2, 3: before_3, 4: before_4}
    after = {4: after_4, 5: after_5, 7: after_7}

    def body(step, carry):
        for k, action in before.items():
            pl.when(step == k)(action)
        pairs, places = [], []
        for part in range(2):
            n = pick(step, [s[part][0] for s in STEPS])
            t = pick(step, [s[part][1] for s in STEPS])
            own = [grids[n, h] for h in range(2)]
            for g in (jnp.where(t == 0, 0, FAR + t), SIB + t):
                pairs.append((own, [grids[g, h] for h in range(2)]))
            places.append(n)
        values = potentials(pairs, tables, coulomb_ref)
        for part, n in enumerate(places):
            for h in range(2):
                first, second = 2 * part, 2 * part + 1
                fields[n, h] += values[first][h] * pairs[first][1][h] + values[second][h] * pairs[second][1][h]
        for k, action in after.items():
            pl.when(step == k)(action)
        return carry

    lax.fori_loop(0, len(STEPS), body, 0)

    received(back[1])
    received(back[3])
    halves = []
    for h in range(2):
        half = fields[0, h, :ROWS] + others[0, h, :ROWS] + others[1, h, :ROWS]
        halves.append(jnp.concatenate([half, jnp.zeros((FULL - ROWS, HALF), F32)], 0))
    hi, lo = split(jnp.concatenate(halves, 1))
    ordered = mm_t(tables[PLACE_T], hi) + mm_t(tables[PLACE_T], lo)
    hi, lo = split(ordered)
    ordered = mm(hi, tables[PLACE]) + mm(lo, tables[PLACE])
    out_ref[0] = ordered[:N, :N]

    def sent(parts):
        for part in parts:
            part.wait_send()

    sent(onward)
    pl.when(is_head)(functools.partial(sent, relay))
    pl.when(jnp.logical_not(is_head))(from_lower[2].wait_send)
    pl.when(x == 2)(from_upper[2].wait_send)
    for copy in copies:
        copy.wait_send()


def on_device(stick_coef, stick_list):
    tables, coulomb = make_tables()
    tables = jnp.asarray(tables.reshape(10, FULL, FULL))
    dma = pltpu.SemaphoreType.DMA
    return pl.pallas_call(
        kernel,
        out_shape=jax.ShapeDtypeStruct((1, N, N), F32),
        in_specs=[pl.BlockSpec(memory_space=pltpu.HBM)] * 4,
        out_specs=pl.BlockSpec(memory_space=pltpu.VMEM),
        scratch_shapes=[
            pltpu.VMEM((SLOTS, BANDS * N), F32),
            pltpu.VMEM((1, SLOTS), jnp.int32),
            pltpu.VMEM((10, FULL, FULL), BF16),
            pltpu.VMEM((FULL, FULL), F32),
            pltpu.VMEM((BANDS, 2, CHUNK, HALF), F32),
            pltpu.VMEM((BANDS, 2, CHUNK, HALF), F32),
            pltpu.VMEM((4, 2 * FULL, HALF), BF16),
            pltpu.VMEM((VIA + 1, 2, FULL, HALF), F32),
            pltpu.VMEM((4, 2, FULL, HALF), F32),
            pltpu.VMEM((3, 2, FULL, HALF), F32),
            dma((5,)),
            dma((84,)),
            dma((84,)),
        ],
        compiler_params=pltpu.CompilerParams(
            collective_id=0, has_side_effects=True, vmem_limit_bytes=40 * 1024 * 1024
        ),
    )(*(pltpu.with_memory_space_constraint(v, pltpu.HBM) for v in (stick_coef, stick_list.reshape(1, SLOTS), tables, jnp.asarray(coulomb))))


def solution(mesh):
    in_specs = (P("plane", "band"), P("plane"))
    out_specs = P(("band", "plane"), None, None)
    return jax.shard_map(on_device, mesh=mesh, in_specs=in_specs, out_specs=out_specs, check_vma=False)
```
